32 devices in a mesh: dp: 4 (over y, x), ctx: 4 (over z), mp: 2 (over core).
Axes of the slice: x: 2, y: 2, z: 4, core: 2. Of those that a mesh axis runs over, the one named last changes fastest.
Arguments:
- streams: bfloat16 [2048, 3, 1536], P(('dp', 'ctx'), None, 'mp'), parts along dimension 0, may hold values from -6 to 6
- short_taps: float32 [7, 3, 96], P(None, None, 'mp'), may hold values from -2.5 to 2.5
- modal_residue: float32 [16, 96], P(None, 'mp'), may hold values from -0.09 to 0.09
- modal_rate: float32 [16, 96], P(None, 'mp'), may hold values from 9.765625e-05 to 0.03
- skip_gain: float32 [1536], P('mp'), may hold values from -4 to 4
- queries: bfloat16 [2048, 16, 128], P(('dp', 'ctx'), 'mp'), parts along dimension 0, may hold values from -9 to 9
- keys: bfloat16 [2048, 2, 128], P(('dp', 'ctx'), 'mp'), parts along dimension 0, may hold values from -9 to 9
- values: bfloat16 [2048, 2, 128], P(('dp', 'ctx'), 'mp'), parts along dimension 0, may hold values from -6 to 6
Outputs:
- hyena_out: bfloat16 [2048, 1536], P(('dp', 'ctx'), 'mp'), parts along dimension 0
- attn_out: bfloat16 [2048, 16, 128], P(('dp', 'ctx'), 'mp'), parts along dimension 0
The draws below stay inside these ranges and needn't reach their ends.
There are 4 independent parts, one for each index of `dp`. The reference program is written for one: setup_inputs(seed, part) draws one part's arguments, and reference() takes and returns one part's arrays. A program takes and returns all parts, laid end to end along the dimension named above; an argument that names none is the same for every part. Nothing has to cross between parts.
All inputs are finite; a program needn't handle non-finite values.
Results may differ from the reference program's by a relative error of at most 0.01.
Values may be sent and summed in bfloat16 or wider, within the bound.
A program may use at most 64 MiB of HBM per device.

```python
import math
import jax
import jax.numpy as jnp
from jax import lax

GSIZE = 16
TAPS = 7
MODES = 16
HD = 128
GROUP = 8
LEN = 512
CHANNELS = 1536
GROUPS = 96
HEADS = 16
KV_HEADS = 2


def query_key_pair(key):
    parts = jax.random.split(jax.random.fold_in(key, 7), 2)
    query_draw = jnp.clip(3.0 * jax.random.normal(parts[0], (LEN, HEADS, HD), jnp.float32), -9.0, 9.0)
    key_draw = jnp.clip(jax.random.normal(parts[1], (LEN, KV_HEADS, HD), jnp.float32), -6.0, 6.0)
    return (query_draw, key_draw)


def draw_queries(key, part):
    return query_key_pair(key)[0].astype(jnp.bfloat16)


def draw_keys(key, part):
    return query_key_pair(key)[1].astype(jnp.bfloat16)


def steps_of(key, extent, cuts, low, high):
    loudness, own = 1.0, jax.random.fold_in(key, 6)
    for dim, blocks in cuts:
        heights = jnp.exp(jax.random.uniform(jax.random.fold_in(own, dim), (blocks,), jnp.float32, low / len(cuts), high / len(cuts)))
        loudness = loudness * jnp.repeat(heights, extent[dim] // blocks).reshape([-1 if axis == dim else 1 for axis in range(len(extent))])
    return loudness


def bell_draw(stream_key, dims, deviation, limit, shards=(), held_as=jnp.bfloat16):
    drawn = jax.random.normal(stream_key, dims, jnp.float32) * deviation
    if len(shards) > 0:
        drawn = steps_of(stream_key, dims, shards, -0.22, 0.18) * drawn
    return jnp.clip(drawn, min=-limit, max=limit).astype(held_as)


def setup_inputs(seed: int = 0, part: int = 0) -> dict:
    streams_of = jax.random.split(jax.random.key(seed), 9)
    own_keys = jax.random.split(jax.random.fold_in(streams_of[8], part), 9)
    streams = bell_draw(own_keys[0], (LEN, 3, CHANNELS), 1.0, 6.0, ((0, 4), (2, 2)))
    short_taps = bell_draw(streams_of[1], (TAPS, 3, GROUPS), 0.3, 2.5, ((2, 2),), jnp.float32)
    modal_residue = bell_draw(streams_of[2], (MODES, GROUPS), 0.015, 0.09, ((1, 2),), jnp.float32)
    modal_rate = jnp.clip(jnp.exp(math.log(0.03) - 5.727499 * jax.random.uniform(streams_of[3], (MODES, GROUPS), jnp.float32) ** steps_of(streams_of[3], (MODES, GROUPS), ((1, 2),), -0.2, 0.2)), 9.765625145519152e-05, 0.03)
    skip_gain = bell_draw(streams_of[4], (CHANNELS,), 1.0, 4.0, ((0, 2),), jnp.float32)
    queries = draw_queries(jax.random.fold_in(jax.random.fold_in(streams_of[8], part), 71), part)
    keys = draw_keys(jax.random.fold_in(jax.random.fold_in(streams_of[8], part), 71), part)
    values = bell_draw(own_keys[7], (LEN, KV_HEADS, HD), 1.0, 6.0, ((0, 4), (1, 2)))
    return dict(streams=streams, short_taps=short_taps, modal_residue=modal_residue, modal_rate=modal_rate, skip_gain=skip_gain, queries=queries, keys=keys, values=values)


def short_filter(streams, short_taps):
    taps_full = jnp.repeat(short_taps, GSIZE, axis=2)
    padded = jnp.pad(streams.astype(jnp.float32), ((TAPS - 1, 0), (0, 0), (0, 0)))
    filtered = jnp.zeros(streams.shape, jnp.float32)
    for offset in range(TAPS):
        filtered = filtered + taps_full[offset] * padded[TAPS - 1 - offset:TAPS - 1 - offset + LEN]
    return filtered

def attend_head(operands):
    query_head, key_head, value_head = operands
    block = min(512, LEN)
    count = LEN // block
    scale = 1.0 / math.sqrt(HD)
    positions = jnp.arange(LEN, dtype=jnp.int32)
    key_float = key_head.astype(jnp.float32)
    value_float = value_head.astype(jnp.float32)
    query_blocks = query_head.reshape(count, block, GROUP, HD)

    def one_block(item):
        query_block, number = item
        scores = jnp.einsum('thd,sd->hts', query_block.astype(jnp.float32), key_float) * scale
        target = number * block + jnp.arange(block, dtype=jnp.int32)
        visible = positions[None, None, :] <= target[None, :, None]
        masked = jnp.where(visible, scores, -1e+30)
        largest = lax.optimization_barrier(jnp.max(masked, axis=-1, keepdims=True))
        weights = jnp.where(visible, jnp.exp(scores - largest), 0.0)
        total = lax.optimization_barrier(jnp.sum(weights, axis=-1))
        rounded = lax.optimization_barrier(weights.astype(jnp.bfloat16))
        mixed = jnp.einsum('hts,sd->htd', rounded.astype(jnp.float32), value_float)
        return (mixed / total[..., None]).astype(jnp.bfloat16)
    result = lax.map(one_block, (query_blocks, jnp.arange(count, dtype=jnp.int32)))
    return jnp.transpose(result, (0, 2, 1, 3)).reshape(LEN, GROUP, HD)

def reference(streams, short_taps, modal_residue, modal_rate, skip_gain, queries, keys, values):
    filtered = short_filter(streams, short_taps)
    gated = (filtered[:, 1] * filtered[:, 2]).astype(jnp.bfloat16)
    lags = jnp.arange(LEN, dtype=jnp.float32)
    table = lax.optimization_barrier(jnp.sum(modal_residue[:, None, :] * jnp.exp(-modal_rate[:, None, :] * lags[None, :, None]), axis=0))
    table_full = jnp.repeat(table, GSIZE, axis=1)
    length = 2 * LEN
    spectrum = jnp.fft.rfft(gated.astype(jnp.float32), n=length, axis=0) * jnp.fft.rfft(table_full, n=length, axis=0)
    long_term = jnp.fft.irfft(spectrum, n=length, axis=0)[:LEN]
    hyena_out = (filtered[:, 0] * (long_term + skip_gain * gated.astype(jnp.float32))).astype(jnp.bfloat16)
    query_heads = jnp.transpose(queries.reshape(LEN, KV_HEADS, GROUP, HD), (1, 0, 2, 3))
    key_heads = jnp.transpose(keys, (1, 0, 2))
    value_heads = jnp.transpose(values, (1, 0, 2))
    mixed = lax.map(attend_head, (query_heads, key_heads, value_heads))
    attn_out = jnp.transpose(mixed, (1, 0, 2, 3)).reshape(LEN, HEADS, HD)
    return (hyena_out, attn_out)
```

```python
import functools
import math

import jax
import jax.numpy as jnp
from jax import lax
from jax.experimental import pallas as pl
from jax.experimental.pallas import tpu as pltpu
from jax.sharding import PartitionSpec as P

GSIZE = 16
LANES = 128
EDGE = 8
HEAD_ROWS = 16
MESH = pl.DeviceIdType.MESH
BF16 = jnp.bfloat16
F32 = jnp.float32


def iota(shape, axis):
    return lax.broadcasted_iota(jnp.int32, shape, axis)


def dot(a, b):
    return jnp.dot(a, b, preferred_element_type=F32)


def dot_nt(a, b):
    return lax.dot_general(a, b, (((1,), (1,)), ((), ())), preferred_element_type=F32)


def split_hi_lo(value):
    high = value.astype(BF16)
    return high, (value - high.astype(F32)).astype(BF16)


def kernel(
    n, heads, chunk,
    streams, taps, residue, rate, skip, q_in, k_in, v_in,
    hy_out, at_out,
    xs, qv, kv, rim_tx, rim_rx, ext, gated, tapx, decay, coeff, toep, longt, gate,
    st_tx, st_rx, acc, big, hy_v, at_v,
    in_sem, out_sem, kv_send, kv_recv, rim_send, rim_recv, st_send, st_recv,
):
    me = lax.axis_index("ctx")
    rows, chans = xs.shape[1], xs.shape[2]
    modes, groups = rate.shape
    reach = taps.shape[1] - 1
    tiles = chans // LANES
    per = LANES // GSIZE
    half = chans // 2

    in_copies = [
        pltpu.make_async_copy(streams, xs, in_sem.at[0]),
        pltpu.make_async_copy(k_in, kv.at[me, 0], in_sem.at[1]),
        pltpu.make_async_copy(v_in, kv.at[me, 1], in_sem.at[2]),
        pltpu.make_async_copy(q_in, qv, in_sem.at[3]),
    ]
    for copy in in_copies:
        copy.start()

    barrier = pltpu.get_barrier_semaphore()
    for d in range(1, n):
        @pl.when(me >= d)
        def _():
            pl.semaphore_signal(barrier, inc=1, device_id={"ctx": me - d}, device_id_type=MESH)

    def kv_copy(part, d):
        src = k_in if part == 0 else v_in
        return pltpu.make_async_remote_copy(
            src_ref=src, dst_ref=kv.at[me, part], send_sem=kv_send.at[d, part],
            recv_sem=kv_recv.at[me, part], device_id={"ctx": me + d}, device_id_type=MESH)

    def kv_arrival(part, source):
        return pltpu.make_async_remote_copy(
            src_ref=kv.at[source, part], dst_ref=kv.at[source, part], send_sem=kv_send.at[0, part],
            recv_sem=kv_recv.at[source, part], device_id={"ctx": source}, device_id_type=MESH)

    def st_copy(d):
        return pltpu.make_async_remote_copy(
            src_ref=st_tx, dst_ref=st_rx.at[me], send_sem=st_send.at[d],
            recv_sem=st_recv.at[me], device_id={"ctx": me + d}, device_id_type=MESH)

    def st_arrival(source):
        return pltpu.make_async_remote_copy(
            src_ref=st_tx, dst_ref=st_rx.at[source], send_sem=st_send.at[0],
            recv_sem=st_recv.at[source], device_id={"ctx": source}, device_id_type=MESH)

    def rim_copy():
        return pltpu.make_async_remote_copy(
            src_ref=rim_tx, dst_ref=rim_rx, send_sem=rim_send, recv_sem=rim_recv,
            device_id={"ctx": lax.rem(me + 1, n)}, device_id_type=MESH)

    in_copies[0].wait()
    tail = xs[:, rows - HEAD_ROWS:, :].astype(F32)[:, HEAD_ROWS - EDGE:, :]
    rim_tx[:, :chans] = jnp.concatenate([tail[1], tail[2]], axis=0).astype(BF16)
    rim_tx[:, chans:] = jnp.concatenate([tail[0, :, :half], tail[0, :, half:]], axis=0).astype(BF16)

    @pl.when(me < n - 1)
    def _():
        pl.semaphore_wait(barrier, n - 1 - me)
        rim_copy().start()

    for d in range(1, n):
        @pl.when(me + d < n)
        def _():
            kv_copy(0, d).start()
            kv_copy(1, d).start()

    spread = (iota((groups, chans), 1) // GSIZE == iota((groups, chans), 0)).astype(F32)
    highest = lax.Precision.HIGHEST
    for j in range(3):
        tapx[j, : reach + 1, :] = jnp.dot(
            taps[j], spread, precision=highest, preferred_element_type=F32)
    rate_nc = jnp.dot(rate[...], spread, precision=highest, preferred_element_type=F32)
    step_decay = jnp.exp(rate_nc * (-float(rows)))

    for j in range(3):
        for q in range(tiles):
            ext[j * tiles + q, EDGE:, :] = xs[j, :, q * LANES:(q + 1) * LANES].astype(F32)

    def filtered(j, q, low, high):
        total = None
        for k in range(reach + 1):
            term = (tapx[j, k:k + 1, q * LANES:(q + 1) * LANES]
                    * ext[j * tiles + q, pl.ds(EDGE - k + low, high - low), :])
            total = term if total is None else total + term
        return total

    def fill_gated(low, high):
        for q in range(tiles):
            gated[low:high, q * LANES:(q + 1) * LANES] = (
                filtered(1, q, low, high) * filtered(2, q, low, high)).astype(BF16)

    fill_gated(HEAD_ROWS, rows)

    lane = iota((modes, LANES), 1).astype(F32)
    causal = iota((rows, LANES), 1) <= iota((rows, LANES), 0)
    rate_v = rate[...]
    residue_v = residue[...]
    for g in range(groups):
        rate_b = jnp.broadcast_to(rate_v[:, g:g + 1], (modes, LANES))
        residue_b = jnp.broadcast_to(residue_v[:, g:g + 1], (modes, LANES))
        fall = jnp.exp(rate_b * (lane - (rows - 1.0)))
        high, low = split_hi_lo(fall)
        q, gg = g // per, g % per
        decay[q, gg * modes:(gg + 1) * modes, :] = high
        decay[q, LANES + gg * modes:LANES + (gg + 1) * modes, :] = low
        coeff[q, gg * modes:(gg + 1) * modes, :] = residue_b * jnp.exp(rate_b * (-1.0 - lane))
        table = jnp.sum(residue_b * fall, axis=0, keepdims=True)
        rolled = pltpu.roll(jnp.broadcast_to(table, (rows, LANES)), 1, 1, stride=1, stride_axis=0)
        toep[q, :, gg * LANES:(gg + 1) * LANES] = jnp.where(causal, rolled, 0.0).astype(BF16)

    @pl.when(me > 0)
    def _():
        rim_copy().wait_recv()
        edge = rim_rx[...].astype(F32)
        for q in range(tiles):
            cut = slice(q * LANES, (q + 1) * LANES)
            ext[tiles + q, :EDGE, :] = edge[:EDGE, cut]
            ext[2 * tiles + q, :EDGE, :] = edge[EDGE:, cut]
            place, row = (q, 0) if q < tiles // 2 else (q - tiles // 2, EDGE)
            ext[q, :EDGE, :] = edge[row:row + EDGE, chans + place * LANES:chans + (place + 1) * LANES]

    @pl.when(me == 0)
    def _():
        ext[:, :EDGE, :] = jnp.zeros((3 * tiles, EDGE, LANES), F32)

    fill_gated(0, HEAD_ROWS)

    pick = iota((modes, LANES), 1) // GSIZE
    for q in range(tiles):
        cut = slice(q * LANES, (q + 1) * LANES)
        full = dot(decay[q], gated[:, cut])
        state = jnp.zeros((modes, LANES), F32)
        for gg in range(per):
            both = (full[gg * modes:(gg + 1) * modes]
                    + full[LANES + gg * modes:LANES + (gg + 1) * modes])
            state = jnp.where(pick == gg, both, state)
        st_tx[:, cut] = state

    for d in range(1, n):
        @pl.when(me + d < n)
        def _():
            st_copy(d).start()

    pick_rows = iota((rows, LANES), 1) // GSIZE
    for q in range(tiles):
        cut = slice(q * LANES, (q + 1) * LANES)
        own = gated[:, cut]
        parts = jnp.concatenate(
            [jnp.where(pick_rows == gg, own, jnp.zeros_like(own)) for gg in range(per)], axis=0)
        longt[:, cut] = dot(toep[q], parts) + skip[:, cut] * own.astype(F32)
        gate[:, cut] = filtered(0, q, 0, rows)

    scale = math.log2(math.e) / math.sqrt(LANES)
    for copy in in_copies[1:]:
        copy.wait()
    ones = jnp.ones((rows, LANES), BF16)
    wide = heads * rows

    own_value = jnp.concatenate([kv[me, 1], ones], axis=1)
    own_key = kv[me, 0]
    for c in range(wide // chunk):
        cut = slice(c * chunk, (c + 1) * chunk)
        scores = dot_nt(qv[cut, :], own_key) * scale
        target = (iota((chunk, LANES), 0) + c * chunk) // heads
        scores = jnp.where(iota((chunk, LANES), 1) <= target, scores, -1e30)
        largest = jnp.broadcast_to(jnp.max(scores, axis=1, keepdims=True), (chunk, LANES))
        weights = jnp.exp2(scores - largest).astype(BF16)
        big[cut, :] = largest
        acc[cut, :] = dot(weights, own_value)

    def far_block(d, carry):
        source = me - d
        kv_arrival(0, source).wait_recv()
        kv_arrival(1, source).wait_recv()
        value = jnp.concatenate([kv[source, 1], ones], axis=1)
        key = kv[source, 0]
        for c in range(wide // chunk):
            cut = slice(c * chunk, (c + 1) * chunk)
            scores = dot_nt(qv[cut, :], key) * scale
            before = big[cut, :]
            largest = jnp.maximum(before, jnp.max(scores, axis=1, keepdims=True))
            weights = jnp.exp2(scores - largest).astype(BF16)
            fix = jnp.exp2(before - largest)
            big[cut, :] = largest
            acc[cut, :] = acc[cut, :] * jnp.concatenate([fix, fix], axis=1) + dot(weights, value)
        return carry

    lax.fori_loop(1, me + 1, far_block, 0)

    for c in range(wide // chunk):
        cut = slice(c * chunk, (c + 1) * chunk)
        at_v[cut, :] = (acc[cut, :LANES] / acc[cut, LANES:]).astype(BF16)
    at_copy = pltpu.make_async_copy(at_v, at_out, out_sem.at[0])
    at_copy.start()

    def gather_state(source, state):
        st_arrival(source).wait_recv()
        return state * step_decay + st_rx[source]

    state = lax.fori_loop(0, me, gather_state, jnp.zeros((modes, chans), F32))
    for q in range(tiles):
        cut = slice(q * LANES, (q + 1) * LANES)
        block = jnp.concatenate(
            [jnp.where(pick == gg, state[:, cut], 0.0) for gg in range(per)], axis=0)
        s_high, s_low = split_hi_lo(block)
        c_high, c_low = split_hi_lo(jnp.transpose(coeff[q]))
        far = dot(jnp.concatenate([c_high, c_low, c_high], axis=1),
                  jnp.concatenate([s_high, s_high, s_low], axis=0))
        hy_v[:, cut] = (gate[:, cut] * (longt[:, cut] + far)).astype(BF16)
    hy_copy = pltpu.make_async_copy(hy_v, hy_out, out_sem.at[1])
    hy_copy.start()

    @pl.when(me < n - 1)
    def _():
        rim_copy().wait_send()

    for d in range(1, n):
        @pl.when(me + d < n)
        def _():
            kv_copy(0, d).wait_send()
            kv_copy(1, d).wait_send()
            st_copy(d).wait_send()
    at_copy.wait()
    hy_copy.wait()


def body(n, streams, short_taps, modal_residue, modal_rate, skip_gain, queries, keys, values):
    rows, _, chans = streams.shape
    heads, size = queries.shape[1], queries.shape[2]
    modes, groups = modal_rate.shape
    tiles = chans // LANES
    per = LANES // GSIZE
    wide = heads * rows
    chunk = min(256, wide)
    reach = short_taps.shape[0]
    vmem, hbm = pl.BlockSpec(memory_space=pltpu.VMEM), pl.BlockSpec(memory_space=pl.ANY)
    dma = pltpu.SemaphoreType.DMA
    hyena, attn = pl.pallas_call(
        functools.partial(kernel, n, heads, chunk),
        out_shape=(jax.ShapeDtypeStruct((rows, chans), BF16),
                   jax.ShapeDtypeStruct((wide, size), BF16)),
        in_specs=[hbm, vmem, vmem, vmem, vmem, hbm, hbm, hbm],
        out_specs=(hbm, hbm),
        scratch_shapes=[
            pltpu.VMEM((3, rows, chans), BF16),
            pltpu.VMEM((wide, size), BF16),
            pltpu.VMEM((n, 2, rows, size), BF16),
            pltpu.VMEM((2 * EDGE, chans + chans // 2), BF16),
            pltpu.VMEM((2 * EDGE, chans + chans // 2), BF16),
            pltpu.VMEM((3 * tiles, rows + EDGE, LANES), F32),
            pltpu.VMEM((rows, chans), BF16),
            pltpu.VMEM((3, EDGE, chans), F32),
            pltpu.VMEM((tiles, 2 * LANES, LANES), BF16),
            pltpu.VMEM((tiles, LANES, LANES), F32),
            pltpu.VMEM((tiles, rows, per * LANES), BF16),
            pltpu.VMEM((rows, chans), F32),
            pltpu.VMEM((rows, chans), F32),
            pltpu.VMEM((modes, chans), F32),
            pltpu.VMEM((n, modes, chans), F32),
            pltpu.VMEM((wide, 2 * size), F32),
            pltpu.VMEM((wide, LANES), F32),
            pltpu.VMEM((rows, chans), BF16),
            pltpu.VMEM((wide, size), BF16),
            dma((4,)), dma((2,)), dma((n, 2)), dma((n, 2)),
            dma, dma, dma((n,)), dma((n,)),
        ],
        compiler_params=pltpu.CompilerParams(
            collective_id=0, has_side_effects=True, vmem_limit_bytes=40 * 1024 * 1024),
        name="mixers",
    )(
        jnp.transpose(streams, (1, 0, 2)),
        jnp.transpose(short_taps, (1, 0, 2)),
        modal_residue,
        modal_rate,
        skip_gain.reshape(1, chans),
        queries.reshape(wide, size),
        keys.reshape(rows, size),
        values.reshape(rows, size),
    )
    return hyena, attn.reshape(rows, heads, size)


def solution(mesh):
    in_specs = (
        P(("dp", "ctx"), None, "mp"),
        P(None, None, "mp"),
        P(None, "mp"),
        P(None, "mp"),
        P("mp"),
        P(("dp", "ctx"), "mp", None),
        P(("dp", "ctx"), "mp", None),
        P(("dp", "ctx"), "mp", None),
    )
    out_specs = (P(("dp", "ctx"), "mp"), P(("dp", "ctx"), "mp", None))
    return jax.shard_map(functools.partial(body, mesh.shape["ctx"]), mesh=mesh,
                         in_specs=in_specs, out_specs=out_specs, check_vma=False)
```

```python
import functools
import math

import jax
import jax.numpy as jnp
from jax import lax
from jax.experimental import pallas as pl
from jax.experimental.pallas import tpu as pltpu
from jax.sharding import PartitionSpec as P

GSIZE = 16
LANES = 128
EDGE = 8
HEAD_ROWS = 16
MESH = pl.DeviceIdType.MESH
BF16 = jnp.bfloat16
F32 = jnp.float32


def iota(shape, axis):
    return lax.broadcasted_iota(jnp.int32, shape, axis)


def dot(a, b):
    return jnp.dot(a, b, preferred_element_type=F32)


def dot_nt(a, b):
    return lax.dot_general(a, b, (((1,), (1,)), ((), ())), preferred_element_type=F32)


def split_hi_lo(value):
    high = value.astype(BF16)
    return high, (value - high.astype(F32)).astype(BF16)


def split_f32(value):
    high = value.astype(BF16).astype(F32)
    return high, value - high


def kernel(
    n, heads, chunk,
    streams, taps_in, residue_in, rate_in, skip_in, q_in, k_in, v_in,
    hy_v, at_v,
    taps, residue, rate, skip,
    xs, qv, kv, rim_tx, rim_rx, ext, gated, mixed, tapx, decay, coeff, toep, longt, gate,
    st_tx, st_rx, acc, big,
    in_sem, kv_send, kv_recv, rim_send, rim_recv, st_send, st_recv,
):
    me = lax.axis_index("ctx")
    rows, chans = xs.shape[1], xs.shape[2]
    modes, groups = rate.shape
    reach = taps.shape[1] - 1
    tiles = chans // LANES
    per = LANES // GSIZE
    half = chans // 2

    in_copies = [
        pltpu.make_async_copy(streams, xs, in_sem.at[0]),
        pltpu.make_async_copy(k_in, kv.at[me, 0], in_sem.at[1]),
        pltpu.make_async_copy(v_in, kv.at[me, 1], in_sem.at[2]),
        pltpu.make_async_copy(q_in, qv, in_sem.at[3]),
        pltpu.make_async_copy(rate_in, rate, in_sem.at[4]),
        pltpu.make_async_copy(residue_in, residue, in_sem.at[5]),
        pltpu.make_async_copy(taps_in, taps, in_sem.at[6]),
        pltpu.make_async_copy(skip_in, skip, in_sem.at[7]),
    ]
    for copy in in_copies:
        copy.start()

    barrier = pltpu.get_barrier_semaphore()
    for d in range(1, n):
        @pl.when(me >= d)
        def _():
            pl.semaphore_signal(barrier, inc=1, device_id={"ctx": me - d}, device_id_type=MESH)

    def kv_copy(part, d):
        src = k_in if part == 0 else v_in
        return pltpu.make_async_remote_copy(
            src_ref=src, dst_ref=kv.at[me, part], send_sem=kv_send.at[d, part],
            recv_sem=kv_recv.at[me, part], device_id={"ctx": me + d}, device_id_type=MESH)

    def kv_arrival(part, source):
        return pltpu.make_async_remote_copy(
            src_ref=kv.at[source, part], dst_ref=kv.at[source, part], send_sem=kv_send.at[0, part],
            recv_sem=kv_recv.at[source, part], device_id={"ctx": source}, device_id_type=MESH)

    def st_copy(d):
        return pltpu.make_async_remote_copy(
            src_ref=st_tx, dst_ref=st_rx.at[me], send_sem=st_send.at[d],
            recv_sem=st_recv.at[me], device_id={"ctx": me + d}, device_id_type=MESH)

    def st_arrival(source):
        return pltpu.make_async_remote_copy(
            src_ref=st_tx, dst_ref=st_rx.at[source], send_sem=st_send.at[0],
            recv_sem=st_recv.at[source], device_id={"ctx": source}, device_id_type=MESH)

    def rim_copy():
        return pltpu.make_async_remote_copy(
            src_ref=rim_tx, dst_ref=rim_rx, send_sem=rim_send, recv_sem=rim_recv,
            device_id={"ctx": lax.rem(me + 1, n)}, device_id_type=MESH)

    in_copies[0].wait()
    tail = xs[:, rows - HEAD_ROWS:, :].astype(F32)[:, HEAD_ROWS - EDGE:, :]
    rim_tx[:, :chans] = jnp.concatenate([tail[1], tail[2]], axis=0).astype(BF16)
    rim_tx[:, chans:] = jnp.concatenate([tail[0, :, :half], tail[0, :, half:]], axis=0).astype(BF16)

    @pl.when(me < n - 1)
    def _():
        pl.semaphore_wait(barrier, n - 1 - me)
        rim_copy().start()

    for d in range(1, n):
        @pl.when(me + d < n)
        def _():
            kv_copy(0, d).start()
            kv_copy(1, d).start()

    for copy in in_copies[4:]:
        copy.wait()
    spread = (iota((groups, chans), 1) // GSIZE == iota((groups, chans), 0)).astype(F32)
    spread = spread.astype(BF16)
    mixed[...] = jnp.zeros(mixed.shape, F32)
    for j in range(3):
        mixed[EDGE * j:EDGE * j + reach + 1, :] = taps[j]
    mixed[3 * EDGE:, :] = rate[...]
    whole = mixed[...]
    high, rest = split_f32(whole)
    middle, rest = split_f32(rest)
    count = 3 * EDGE + modes
    spread_out = dot(jnp.concatenate([high, middle, rest], axis=0).astype(BF16), spread)
    spread_out = (spread_out[2 * count:] + spread_out[count:2 * count]) + spread_out[:count]
    for j in range(3):
        tapx[j] = spread_out[EDGE * j:EDGE * (j + 1)]
    rate_nc = spread_out[3 * EDGE:]
    step_decay = jnp.exp(rate_nc * (-float(rows)))

    for j in range(3):
        for q in range(tiles):
            ext[j * tiles + q, EDGE:, :] = xs[j, :, q * LANES:(q + 1) * LANES].astype(F32)

    def filtered(j, q, low, high):
        total = None
        for k in range(reach + 1):
            term = (tapx[j, k:k + 1, q * LANES:(q + 1) * LANES]
                    * ext[j * tiles + q, pl.ds(EDGE - k + low, high - low), :])
            total = term if total is None else total + term
        return total

    def fill_gated(low, high):
        for q in range(tiles):
            gated[low:high, q * LANES:(q + 1) * LANES] = (
                filtered(1, q, low, high) * filtered(2, q, low, high)).astype(BF16)

    fill_gated(HEAD_ROWS, rows)

    lane = iota((modes, LANES), 1).astype(F32)
    causal = iota((rows, LANES), 1) <= iota((rows, LANES), 0)
    rate_v = rate[...]
    residue_v = residue[...]
    for g in range(groups):
        rate_b = jnp.broadcast_to(rate_v[:, g:g + 1], (modes, LANES))
        residue_b = jnp.broadcast_to(residue_v[:, g:g + 1], (modes, LANES))
        fall = jnp.exp(rate_b * (lane - (rows - 1.0)))
        high, low = split_hi_lo(fall)
        q, gg = g // per, g % per
        decay[q, gg * modes:(gg + 1) * modes, :] = high
        decay[q, LANES + gg * modes:LANES + (gg + 1) * modes, :] = low
        coeff[q, gg * modes:(gg + 1) * modes, :] = residue_b * jnp.exp(rate_b * (-1.0 - lane))
        table = jnp.sum(residue_b * fall, axis=0, keepdims=True)
        rolled = pltpu.roll(jnp.broadcast_to(table, (rows, LANES)), 1, 1, stride=1, stride_axis=0)
        toep[q, :, gg * LANES:(gg + 1) * LANES] = jnp.where(causal, rolled, 0.0).astype(BF16)

    @pl.when(me > 0)
    def _():
        rim_copy().wait_recv()
        edge = rim_rx[...].astype(F32)
        for q in range(tiles):
            cut = slice(q * LANES, (q + 1) * LANES)
            ext[tiles + q, :EDGE, :] = edge[:EDGE, cut]
            ext[2 * tiles + q, :EDGE, :] = edge[EDGE:, cut]
            place, row = (q, 0) if q < tiles // 2 else (q - tiles // 2, EDGE)
            ext[q, :EDGE, :] = edge[row:row + EDGE, chans + place * LANES:chans + (place + 1) * LANES]

    @pl.when(me == 0)
    def _():
        ext[:, :EDGE, :] = jnp.zeros((3 * tiles, EDGE, LANES), F32)

    fill_gated(0, HEAD_ROWS)

    pick = iota((modes, LANES), 1) // GSIZE
    for q in range(tiles):
        cut = slice(q * LANES, (q + 1) * LANES)
        full = dot(decay[q], gated[:, cut])
        state = jnp.zeros((modes, LANES), F32)
        for gg in range(per):
            both = (full[gg * modes:(gg + 1) * modes]
                    + full[LANES + gg * modes:LANES + (gg + 1) * modes])
            state = jnp.where(pick == gg, both, state)
        st_tx[:, cut] = state

    for d in range(1, n):
        @pl.when(me + d < n)
        def _():
            st_copy(d).start()

    picks = [(iota((1, LANES), 1) // GSIZE == gg).astype(F32).astype(BF16) for gg in range(per)]
    for q in range(tiles):
        cut = slice(q * LANES, (q + 1) * LANES)
        own = gated[:, cut]
        parts = jnp.concatenate([own * picks[gg] for gg in range(per)], axis=0)
        skip_row = skip[cut].reshape(1, LANES)
        longt[:, cut] = dot(toep[q], parts) + skip_row * own.astype(F32)
        gate[:, cut] = filtered(0, q, 0, rows)

    scale = math.log2(math.e) / math.sqrt(LANES)
    for copy in in_copies[1:4]:
        copy.wait()
    ones = jnp.ones((HEAD_ROWS, rows), BF16)
    wide = heads * rows
    last = LANES + EDGE

    def values_of(source):
        turned = jnp.transpose(kv[source, 1].astype(F32)).astype(BF16)
        return jnp.concatenate([turned, ones], axis=0)

    own_value = values_of(me)
    for c in range(wide // chunk):
        cut = slice(c * chunk, (c + 1) * chunk)
        seen = (c + 1) * chunk // heads
        scores = dot_nt(kv[me, 0, :seen, :], qv[cut, :])
        target = (iota((seen, chunk), 1) + c * chunk) // heads
        scores = jnp.where(iota((seen, chunk), 0) <= target, scores, -1e30)
        largest = jnp.max(scores, axis=0, keepdims=True)
        weights = jnp.exp2((scores - largest) * scale).astype(BF16)
        big[:, cut] = jnp.broadcast_to(largest, (EDGE, chunk))
        acc[:, cut] = dot(own_value[:, :seen], weights)[:last]

    def far_block(d, carry):
        source = me - d
        kv_arrival(0, source).wait_recv()
        kv_arrival(1, source).wait_recv()
        value = values_of(source)
        for c in range(wide // chunk):
            cut = slice(c * chunk, (c + 1) * chunk)
            scores = dot_nt(kv[source, 0], qv[cut, :])
            before = big[:1, cut]
            largest = jnp.maximum(before, jnp.max(scores, axis=0, keepdims=True))
            weights = jnp.exp2((scores - largest) * scale).astype(BF16)
            fix = jnp.exp2((before - largest) * scale)
            big[:, cut] = jnp.broadcast_to(largest, (EDGE, chunk))
            acc[:, cut] = acc[:, cut] * fix + dot(value, weights)[:last]
        return carry

    lax.fori_loop(1, me + 1, far_block, 0)

    for c in range(wide // LANES):
        cut = slice(c * LANES, (c + 1) * LANES)
        ratio = acc[:LANES, cut] * (1.0 / acc[LANES:LANES + 1, cut])
        at_v[cut, :] = jnp.transpose(ratio).astype(BF16)

    def gather_state(source, state):
        st_arrival(source).wait_recv()
        return state * step_decay + st_rx[source]

    state = lax.fori_loop(0, me, gather_state, jnp.zeros((modes, chans), F32))
    for q in range(tiles):
        cut = slice(q * LANES, (q + 1) * LANES)
        block = jnp.concatenate(
            [jnp.where(pick == gg, state[:, cut], 0.0) for gg in range(per)], axis=0)
        s_high, s_low = split_hi_lo(block)
        c_high, c_low = split_hi_lo(jnp.transpose(coeff[q]))
        far = dot(jnp.concatenate([c_high, c_low, c_high], axis=1),
                  jnp.concatenate([s_high, s_high, s_low], axis=0))
        hy_v[:, cut] = (gate[:, cut] * (longt[:, cut] + far)).astype(BF16)

    @pl.when(me < n - 1)
    def _():
        rim_copy().wait_send()

    for d in range(1, n):
        @pl.when(me + d < n)
        def _():
            kv_copy(0, d).wait_send()
            kv_copy(1, d).wait_send()
            st_copy(d).wait_send()


def leave(hy_v, at_v, hy_out, at_out, sem):
    copies = [pltpu.make_async_copy(hy_v, hy_out, sem.at[0]),
              pltpu.make_async_copy(at_v, at_out, sem.at[1])]
    for copy in copies:
        copy.start()
    for copy in copies:
        copy.wait()


def body(n, streams, short_taps, modal_residue, modal_rate, skip_gain, queries, keys, values):
    rows, _, chans = streams.shape
    heads, size = queries.shape[1], queries.shape[2]
    modes, groups = modal_rate.shape
    tiles = chans // LANES
    per = LANES // GSIZE
    wide = heads * rows
    chunk = min(256, wide)
    reach = short_taps.shape[0]
    vmem, hbm = pl.BlockSpec(memory_space=pltpu.VMEM), pl.BlockSpec(memory_space=pltpu.HBM)
    dma = pltpu.SemaphoreType.DMA
    hyena, attn = pl.pallas_call(
        functools.partial(kernel, n, heads, chunk),
        out_shape=(jax.ShapeDtypeStruct((rows, chans), BF16),
                   jax.ShapeDtypeStruct((wide, size), BF16)),
        in_specs=[hbm] * 8,
        out_specs=(vmem, vmem),
        scratch_shapes=[
            pltpu.VMEM((3, reach, groups), F32),
            pltpu.VMEM((modes, groups), F32),
            pltpu.VMEM((modes, groups), F32),
            pltpu.VMEM((chans,), F32),
            pltpu.VMEM((3, rows, chans), BF16),
            pltpu.VMEM((wide, size), BF16),
            pltpu.VMEM((n, 2, rows, size), BF16),
            pltpu.VMEM((2 * EDGE, chans + chans // 2), BF16),
            pltpu.VMEM((2 * EDGE, chans + chans // 2), BF16),
            pltpu.VMEM((3 * tiles, rows + EDGE, LANES), F32),
            pltpu.VMEM((rows, chans), BF16),
            pltpu.VMEM((3 * EDGE + modes, groups), F32),
            pltpu.VMEM((3, EDGE, chans), F32),
            pltpu.VMEM((tiles, 2 * LANES, LANES), BF16),
            pltpu.VMEM((tiles, LANES, LANES), F32),
            pltpu.VMEM((tiles, rows, per * LANES), BF16),
            pltpu.VMEM((rows, chans), F32),
            pltpu.VMEM((rows, chans), F32),
            pltpu.VMEM((modes, chans), F32),
            pltpu.VMEM((n, modes, chans), F32),
            pltpu.VMEM((size + EDGE, wide), F32),
            pltpu.VMEM((EDGE, wide), F32),
            dma((8,)), dma((n, 2)), dma((n, 2)),
            dma, dma, dma((n,)), dma((n,)),
        ],
        compiler_params=pltpu.CompilerParams(
            collective_id=0, has_side_effects=True, vmem_limit_bytes=40 * 1024 * 1024),
        name="mixers",
    )(*[pltpu.with_memory_space_constraint(x, pltpu.HBM) for x in (
        jnp.transpose(streams, (1, 0, 2)),
        jnp.transpose(short_taps, (1, 0, 2)),
        modal_residue,
        modal_rate,
        skip_gain,
        queries.reshape(wide, size),
        keys.reshape(rows, size),
        values.reshape(rows, size),
    )])
    hyena, attn = pl.pallas_call(
        leave,
        out_shape=(jax.ShapeDtypeStruct((rows, chans), BF16),
                   jax.ShapeDtypeStruct((wide, size), BF16)),
        in_specs=[vmem, vmem],
        out_specs=(hbm, hbm),
        scratch_shapes=[dma((2,))],
        name="leave",
    )(hyena, attn)
    return hyena, attn.reshape(rows, heads, size)


def solution(mesh):
    in_specs = (
        P(("dp", "ctx"), None, "mp"),
        P(None, None, "mp"),
        P(None, "mp"),
        P(None, "mp"),
        P("mp"),
        P(("dp", "ctx"), "mp", None),
        P(("dp", "ctx"), "mp", None),
        P(("dp", "ctx"), "mp", None),
    )
    out_specs = (P(("dp", "ctx"), "mp"), P(("dp", "ctx"), "mp", None))
    return jax.shard_map(functools.partial(body, mesh.shape["ctx"]), mesh=mesh,
                         in_specs=in_specs, out_specs=out_specs, check_vma=False)
```

```python
import functools
import math

import jax
import jax.numpy as jnp
from jax import lax
from jax.experimental import pallas as pl
from jax.experimental.pallas import tpu as pltpu
from jax.sharding import PartitionSpec as P

GSIZE = 16
LANES = 128
EDGE = 8
HEAD_ROWS = 16
MESH = pl.DeviceIdType.MESH
BF16 = jnp.bfloat16
F32 = jnp.float32


def iota(shape, axis):
    return lax.broadcasted_iota(jnp.int32, shape, axis)


def dot(a, b):
    return jnp.dot(a, b, preferred_element_type=F32)


def dot_nt(a, b):
    return lax.dot_general(a, b, (((1,), (1,)), ((), ())), preferred_element_type=F32)


def split_f32(value):
    high = value.astype(BF16).astype(F32)
    return high, value - high


def kernel(
    n, heads, chunk,
    streams, taps_in, residue_in, rate_in, skip_in, q_in, k_in, v_in,
    hy_v, at_v,
    taps, residue, rate, skip,
    xs, qv, kv, rim_tx, rim_rx, ext, gated, mixed, tapx, falls, decay, coeff, toep, longt, gate,
    st_tx, st_rx, acc, big,
    in_sem, kv_send, kv_recv, rim_send, rim_recv, st_send, st_recv,
):
    me = lax.axis_index("ctx")
    rows, chans = xs.shape[1], xs.shape[2]
    modes, groups = rate.shape
    reach = taps.shape[1] - 1
    tiles = chans // LANES
    per = LANES // GSIZE
    half = chans // 2

    in_copies = [
        pltpu.make_async_copy(streams, xs, in_sem.at[0]),
        pltpu.make_async_copy(k_in, kv.at[me, 0], in_sem.at[1]),
        pltpu.make_async_copy(v_in, kv.at[me, 1], in_sem.at[2]),
        pltpu.make_async_copy(q_in, qv, in_sem.at[3]),
        pltpu.make_async_copy(rate_in, rate, in_sem.at[4]),
        pltpu.make_async_copy(residue_in, residue, in_sem.at[5]),
        pltpu.make_async_copy(taps_in, taps, in_sem.at[6]),
        pltpu.make_async_copy(skip_in, skip, in_sem.at[7]),
    ]
    for copy in in_copies:
        copy.start()

    barrier = pltpu.get_barrier_semaphore()
    for d in range(1, n):
        @pl.when(me >= d)
        def _():
            pl.semaphore_signal(barrier, inc=1, device_id={"ctx": me - d}, device_id_type=MESH)

    def kv_copy(part, source, d, own=False):
        src = (k_in if part == 0 else v_in) if own else kv.at[source, part]
        return pltpu.make_async_remote_copy(
            src_ref=src, dst_ref=kv.at[source, part], send_sem=kv_send.at[source, d - 1, part],
            recv_sem=kv_recv.at[source, part], device_id={"ctx": me + d}, device_id_type=MESH)

    def kv_each(source, own, act):
        for d in (1, 2):
            @pl.when(me + d < n)
            def _():
                act(kv_copy(0, source, d, own))
                act(kv_copy(1, source, d, own))

    def kv_arrival(part, source):
        return pltpu.make_async_remote_copy(
            src_ref=kv.at[source, part], dst_ref=kv.at[source, part], send_sem=kv_send.at[source, 0, part],
            recv_sem=kv_recv.at[source, part], device_id={"ctx": source}, device_id_type=MESH)

    def st_copy(d):
        return pltpu.make_async_remote_copy(
            src_ref=st_tx, dst_ref=st_rx.at[me], send_sem=st_send.at[d],
            recv_sem=st_recv.at[me], device_id={"ctx": me + d}, device_id_type=MESH)

    def st_arrival(source):
        return pltpu.make_async_remote_copy(
            src_ref=st_tx, dst_ref=st_rx.at[source], send_sem=st_send.at[0],
            recv_sem=st_recv.at[source], device_id={"ctx": source}, device_id_type=MESH)

    def rim_copy():
        return pltpu.make_async_remote_copy(
            src_ref=rim_tx, dst_ref=rim_rx, send_sem=rim_send, recv_sem=rim_recv,
            device_id={"ctx": lax.rem(me + 1, n)}, device_id_type=MESH)

    in_copies[0].wait()
    tail = xs[:, rows - HEAD_ROWS:, :].astype(F32)[:, HEAD_ROWS - EDGE:, :]
    rim_tx[:, :chans] = jnp.concatenate([tail[1], tail[2]], axis=0).astype(BF16)
    rim_tx[:, chans:] = jnp.concatenate([tail[0, :, :half], tail[0, :, half:]], axis=0).astype(BF16)

    @pl.when(me < n - 1)
    def _():
        pl.semaphore_wait(barrier, n - 1 - me)
        rim_copy().start()

    kv_each(me, True, lambda copy: copy.start())

    for copy in in_copies[4:]:
        copy.wait()
    spread = (iota((groups, chans), 1) // GSIZE == iota((groups, chans), 0)).astype(F32)
    spread = spread.astype(BF16)
    mixed[...] = jnp.zeros(mixed.shape, F32)
    for j in range(3):
        mixed[EDGE * j:EDGE * j + reach + 1, :] = taps[j]
    mixed[3 * EDGE:, :] = rate[...]
    whole = mixed[...]
    high, rest = split_f32(whole)
    middle, rest = split_f32(rest)
    count = 3 * EDGE + modes
    spread_out = dot(jnp.concatenate([high, middle, rest], axis=0).astype(BF16), spread)
    spread_out = (spread_out[2 * count:] + spread_out[count:2 * count]) + spread_out[:count]
    for j in range(3):
        tapx[j] = spread_out[EDGE * j:EDGE * (j + 1)]
    rate_nc = spread_out[3 * EDGE:]
    step_decay = jnp.exp(rate_nc * (-float(rows)))

    for j in range(3):
        for q in range(tiles):
            ext[j * tiles + q, EDGE:, :] = xs[j, :, q * LANES:(q + 1) * LANES].astype(F32)

    def filtered(j, q, low, high):
        total = None
        for k in range(reach + 1):
            term = (tapx[j, k:k + 1, q * LANES:(q + 1) * LANES]
                    * ext[j * tiles + q, pl.ds(EDGE - k + low, high - low), :])
            total = term if total is None else total + term
        return total

    def fill_gated(low, high):
        for q in range(tiles):
            gated[low:high, q * LANES:(q + 1) * LANES] = (
                filtered(1, q, low, high) * filtered(2, q, low, high)).astype(BF16)

    fill_gated(HEAD_ROWS, rows)

    lane = iota((modes, LANES), 1).astype(F32)
    rate_v = rate[...]
    for g in range(groups):
        rate_b = jnp.broadcast_to(rate_v[:, g:g + 1], (modes, LANES))
        fall = jnp.exp(rate_b * (lane - (rows - 1.0)))
        q, gg = g // per, g % per
        falls[q, gg * modes:(gg + 1) * modes, :] = fall
        decay[q, gg * modes:(gg + 1) * modes, :] = fall.astype(BF16)

    @pl.when(me > 0)
    def _():
        rim_copy().wait_recv()
        edge = rim_rx[...].astype(F32)
        for q in range(tiles):
            cut = slice(q * LANES, (q + 1) * LANES)
            ext[tiles + q, :EDGE, :] = edge[:EDGE, cut]
            ext[2 * tiles + q, :EDGE, :] = edge[EDGE:, cut]
            place, row = (q, 0) if q < tiles // 2 else (q - tiles // 2, EDGE)
            ext[q, :EDGE, :] = edge[row:row + EDGE, chans + place * LANES:chans + (place + 1) * LANES]

    @pl.when(me == 0)
    def _():
        ext[:, :EDGE, :] = jnp.zeros((3 * tiles, EDGE, LANES), F32)

    fill_gated(0, HEAD_ROWS)

    pick = iota((modes, LANES), 1) // GSIZE
    for q in range(tiles):
        cut = slice(q * LANES, (q + 1) * LANES)
        full = dot(decay[q], gated[:, cut])
        state = jnp.zeros((modes, LANES), F32)
        for gg in range(per):
            state = jnp.where(pick == gg, full[gg * modes:(gg + 1) * modes], state)
        st_tx[:, cut] = state.astype(BF16)

    for d in range(1, n):
        @pl.when(me + d < n)
        def _():
            st_copy(d).start()

    causal = iota((rows, LANES), 1) <= iota((rows, LANES), 0)
    residue_v = residue[...]
    for q in range(tiles):
        turned = []
        for gg in range(per):
            g = q * per + gg
            rate_b = jnp.broadcast_to(rate_v[:, g:g + 1], (modes, LANES))
            residue_b = jnp.broadcast_to(residue_v[:, g:g + 1], (modes, LANES))
            turned.append(residue_b * jnp.exp(rate_b * (-1.0 - lane)))
            fall = falls[q, gg * modes:(gg + 1) * modes, :]
            table = jnp.sum(residue_b * fall, axis=0, keepdims=True)
            rolled = pltpu.roll(
                jnp.broadcast_to(table, (rows, LANES)), 1, 1, stride=1, stride_axis=0)
            toep[q, :, gg * LANES:(gg + 1) * LANES] = jnp.where(causal, rolled, 0.0).astype(BF16)
        coeff[q] = jnp.transpose(jnp.concatenate(turned, axis=0)).astype(BF16)

    picks = [(iota((1, LANES), 1) // GSIZE == gg).astype(F32).astype(BF16) for gg in range(per)]
    for q in range(tiles):
        cut = slice(q * LANES, (q + 1) * LANES)
        own = gated[:, cut]
        parts = jnp.concatenate([own * picks[gg] for gg in range(per)], axis=0)
        skip_row = skip[cut].reshape(1, LANES)
        longt[:, cut] = dot(toep[q], parts) + skip_row * own.astype(F32)
        gate[:, cut] = filtered(0, q, 0, rows)

    scale = math.log2(math.e) / math.sqrt(LANES)
    for copy in in_copies[1:4]:
        copy.wait()
    ones = jnp.ones((HEAD_ROWS, rows), BF16)
    wide = heads * rows
    last = LANES + EDGE

    def values_of(source):
        turned = jnp.transpose(kv[source, 1].astype(F32)).astype(BF16)
        return jnp.concatenate([turned, ones], axis=0)

    def forward(k, carry):
        source = me - 2 * k
        kv_arrival(0, source).wait_recv()
        kv_arrival(1, source).wait_recv()
        kv_each(source, False, lambda copy: copy.start())
        return carry

    @pl.when(me < n - 1)
    def _():
        lax.fori_loop(1, me // 2 + 1, forward, 0)

    own_value = values_of(me)
    for c in range(wide // chunk):
        cut = slice(c * chunk, (c + 1) * chunk)
        seen = (c + 1) * chunk // heads
        scores = dot_nt(kv[me, 0, :seen, :], qv[cut, :])
        target = (iota((seen, chunk), 1) + c * chunk) // heads
        scores = jnp.where(iota((seen, chunk), 0) <= target, scores, -1e30)
        largest = jnp.max(scores, axis=0, keepdims=True)
        weights = jnp.exp2((scores - largest) * scale).astype(BF16)
        big[:, cut] = jnp.broadcast_to(largest, (EDGE, chunk))
        acc[:, cut] = dot(own_value[:, :seen], weights)[:last]

    def far_block(d, carry):
        source = me - d

        @pl.when((lax.rem(d, 2) == 1) | (me == n - 1))
        def _():
            kv_arrival(0, source).wait_recv()
            kv_arrival(1, source).wait_recv()

        value = values_of(source)
        for c in range(wide // chunk):
            cut = slice(c * chunk, (c + 1) * chunk)
            scores = dot_nt(kv[source, 0], qv[cut, :])
            before = big[:1, cut]
            largest = jnp.maximum(before, jnp.max(scores, axis=0, keepdims=True))
            weights = jnp.exp2((scores - largest) * scale).astype(BF16)
            fix = jnp.exp2((before - largest) * scale)
            big[:, cut] = jnp.broadcast_to(largest, (EDGE, chunk))
            acc[:, cut] = acc[:, cut] * fix + dot(value, weights)[:last]
        return carry

    lax.fori_loop(1, me + 1, far_block, 0)

    for c in range(wide // LANES):
        cut = slice(c * LANES, (c + 1) * LANES)
        ratio = acc[:LANES, cut] * (1.0 / acc[LANES:LANES + 1, cut])
        at_v[cut, :] = jnp.transpose(ratio).astype(BF16)

    def gather_state(source, state):
        st_arrival(source).wait_recv()
        return state * step_decay + st_rx[source].astype(F32)

    state = lax.fori_loop(0, me, gather_state, jnp.zeros((modes, chans), F32))
    for q in range(tiles):
        cut = slice(q * LANES, (q + 1) * LANES)
        block = jnp.concatenate(
            [jnp.where(pick == gg, state[:, cut], 0.0) for gg in range(per)], axis=0)
        far = dot(coeff[q], block.astype(BF16))
        hy_v[:, cut] = (gate[:, cut] * (longt[:, cut] + far)).astype(BF16)

    @pl.when(me < n - 1)
    def _():
        rim_copy().wait_send()

    for d in range(1, n):
        @pl.when(me + d < n)
        def _():
            st_copy(d).wait_send()

    kv_each(me, True, lambda copy: copy.wait_send())

    def forwarded(k, carry):
        kv_each(me - 2 * k, False, lambda copy: copy.wait_send())
        return carry

    lax.fori_loop(1, me // 2 + 1, forwarded, 0)


def leave(hy_v, at_v, hy_out, at_out, sem):
    copies = [pltpu.make_async_copy(hy_v, hy_out, sem.at[0]),
              pltpu.make_async_copy(at_v, at_out, sem.at[1])]
    for copy in copies:
        copy.start()
    for copy in copies:
        copy.wait()


def body(n, streams, short_taps, modal_residue, modal_rate, skip_gain, queries, keys, values):
    rows, _, chans = streams.shape
    heads, size = queries.shape[1], queries.shape[2]
    modes, groups = modal_rate.shape
    tiles = chans // LANES
    per = LANES // GSIZE
    wide = heads * rows
    chunk = min(256, wide)
    reach = short_taps.shape[0]
    vmem, hbm = pl.BlockSpec(memory_space=pltpu.VMEM), pl.BlockSpec(memory_space=pltpu.HBM)
    dma = pltpu.SemaphoreType.DMA
    hyena, attn = pl.pallas_call(
        functools.partial(kernel, n, heads, chunk),
        out_shape=(jax.ShapeDtypeStruct((rows, chans), BF16),
                   jax.ShapeDtypeStruct((wide, size), BF16)),
        in_specs=[hbm] * 8,
        out_specs=(vmem, vmem),
        scratch_shapes=[
            pltpu.VMEM((3, reach, groups), F32),
            pltpu.VMEM((modes, groups), F32),
            pltpu.VMEM((modes, groups), F32),
            pltpu.VMEM((chans,), F32),
            pltpu.VMEM((3, rows, chans), BF16),
            pltpu.VMEM((wide, size), BF16),
            pltpu.VMEM((n, 2, rows, size), BF16),
            pltpu.VMEM((2 * EDGE, chans + chans // 2), BF16),
            pltpu.VMEM((2 * EDGE, chans + chans // 2), BF16),
            pltpu.VMEM((3 * tiles, rows + EDGE, LANES), F32),
            pltpu.VMEM((rows, chans), BF16),
            pltpu.VMEM((3 * EDGE + modes, groups), F32),
            pltpu.VMEM((3, EDGE, chans), F32),
            pltpu.VMEM((tiles, LANES, LANES), F32),
            pltpu.VMEM((tiles, LANES, LANES), BF16),
            pltpu.VMEM((tiles, LANES, LANES), BF16),
            pltpu.VMEM((tiles, rows, per * LANES), BF16),
            pltpu.VMEM((rows, chans), F32),
            pltpu.VMEM((rows, chans), F32),
            pltpu.VMEM((modes, chans), BF16),
            pltpu.VMEM((n, modes, chans), BF16),
            pltpu.VMEM((size + EDGE, wide), F32),
            pltpu.VMEM((EDGE, wide), F32),
            dma((8,)), dma((n, 2, 2)), dma((n, 2)),
            dma, dma, dma((n,)), dma((n,)),
        ],
        compiler_params=pltpu.CompilerParams(
            collective_id=0, has_side_effects=True, vmem_limit_bytes=40 * 1024 * 1024),
        name="mixers",
    )(*[pltpu.with_memory_space_constraint(x, pltpu.HBM) for x in (
        jnp.transpose(streams, (1, 0, 2)),
        jnp.transpose(short_taps, (1, 0, 2)),
        modal_residue,
        modal_rate,
        skip_gain,
        queries.reshape(wide, size),
        keys.reshape(rows, size),
        values.reshape(rows, size),
    )])
    hyena, attn = pl.pallas_call(
        leave,
        out_shape=(jax.ShapeDtypeStruct((rows, chans), BF16),
                   jax.ShapeDtypeStruct((wide, size), BF16)),
        in_specs=[vmem, vmem],
        out_specs=(hbm, hbm),
        scratch_shapes=[dma((2,))],
        compiler_params=pltpu.CompilerParams(vmem_limit_bytes=2 * 1024 * 1024),
        name="leave",
    )(hyena, attn)
    return hyena, attn.reshape(rows, heads, size)


def solution(mesh):
    in_specs = (
        P(("dp", "ctx"), None, "mp"),
        P(None, None, "mp"),
        P(None, "mp"),
        P(None, "mp"),
        P("mp"),
        P(("dp", "ctx"), "mp", None),
        P(("dp", "ctx"), "mp", None),
        P(("dp", "ctx"), "mp", None),
    )
    out_specs = (P(("dp", "ctx"), "mp"), P(("dp", "ctx"), "mp", None))
    return jax.shard_map(functools.partial(body, mesh.shape["ctx"]), mesh=mesh,
                         in_specs=in_specs, out_specs=out_specs, check_vma=False)
```

```python
import functools
import math

import jax
import jax.numpy as jnp
from jax import lax
from jax.experimental import pallas as pl
from jax.experimental.pallas import tpu as pltpu
from jax.sharding import PartitionSpec as P

GSIZE = 16
LANES = 128
EDGE = 8
HEAD_ROWS = 16
MESH = pl.DeviceIdType.MESH
BF16 = jnp.bfloat16
F32 = jnp.float32


def iota(shape, axis):
    return lax.broadcasted_iota(jnp.int32, shape, axis)


def dot(a, b):
    return jnp.dot(a, b, preferred_element_type=F32)


def dot_nt(a, b):
    return lax.dot_general(a, b, (((1,), (1,)), ((), ())), preferred_element_type=F32)


def split_f32(value):
    high = value.astype(BF16).astype(F32)
    return high, value - high


def kernel(
    n, heads, chunk,
    streams, taps_in, residue_in, rate_in, skip_in, q_in, k_in, v_in,
    hy_v, at_v,
    taps, residue, rate, skip,
    xs, qv, kv, rim_tx, rim_rx, ext, gated, mixed, tapx, falls, decay, coeff, toep, longt, gate,
    st_tx, st_rx, acc, big,
    in_sem, kv_send, kv_recv, rim_send, rim_recv, st_send, st_recv,
):
    me = lax.axis_index("ctx")
    rows, chans = xs.shape[1], xs.shape[2]
    modes, groups = rate.shape
    reach = taps.shape[1] - 1
    tiles = chans // LANES
    per = LANES // GSIZE
    half = chans // 2

    in_copies = [
        pltpu.make_async_copy(streams, xs, in_sem.at[0]),
        pltpu.make_async_copy(k_in, kv.at[me, 0], in_sem.at[1]),
        pltpu.make_async_copy(v_in, kv.at[me, 1], in_sem.at[2]),
        pltpu.make_async_copy(q_in, qv, in_sem.at[3]),
        pltpu.make_async_copy(rate_in, rate, in_sem.at[4]),
        pltpu.make_async_copy(residue_in, residue, in_sem.at[5]),
        pltpu.make_async_copy(taps_in, taps, in_sem.at[6]),
        pltpu.make_async_copy(skip_in, skip, in_sem.at[7]),
    ]
    for copy in in_copies:
        copy.start()

    barrier = pltpu.get_barrier_semaphore()
    for d in range(1, n):
        @pl.when(me >= d)
        def _():
            pl.semaphore_signal(barrier, inc=1, device_id={"ctx": me - d}, device_id_type=MESH)

    def kv_copy(part, source, d, own=False):
        src = (k_in if part == 0 else v_in) if own else kv.at[source, part]
        return pltpu.make_async_remote_copy(
            src_ref=src, dst_ref=kv.at[source, part], send_sem=kv_send.at[source, d - 1, part],
            recv_sem=kv_recv.at[source, part], device_id={"ctx": me + d}, device_id_type=MESH)

    def kv_each(source, own, act):
        for d in (2, 1):
            @pl.when(me + d < n)
            def _():
                act(kv_copy(0, source, d, own))
                act(kv_copy(1, source, d, own))

    def kv_arrival(part, source):
        return pltpu.make_async_remote_copy(
            src_ref=kv.at[source, part], dst_ref=kv.at[source, part], send_sem=kv_send.at[source, 0, part],
            recv_sem=kv_recv.at[source, part], device_id={"ctx": source}, device_id_type=MESH)

    def st_copy(d):
        return pltpu.make_async_remote_copy(
            src_ref=st_tx, dst_ref=st_rx.at[me], send_sem=st_send.at[d],
            recv_sem=st_recv.at[me], device_id={"ctx": me + d}, device_id_type=MESH)

    def st_arrival(source):
        return pltpu.make_async_remote_copy(
            src_ref=st_tx, dst_ref=st_rx.at[source], send_sem=st_send.at[0],
            recv_sem=st_recv.at[source], device_id={"ctx": source}, device_id_type=MESH)

    def rim_copy():
        return pltpu.make_async_remote_copy(
            src_ref=rim_tx, dst_ref=rim_rx, send_sem=rim_send, recv_sem=rim_recv,
            device_id={"ctx": lax.rem(me + 1, n)}, device_id_type=MESH)

    in_copies[0].wait()
    tail = xs[:, rows - HEAD_ROWS:, :].astype(F32)[:, HEAD_ROWS - EDGE:, :]
    rim_tx[:, :chans] = jnp.concatenate([tail[1], tail[2]], axis=0).astype(BF16)
    rim_tx[:, chans:] = jnp.concatenate([tail[0, :, :half], tail[0, :, half:]], axis=0).astype(BF16)

    @pl.when(me < n - 1)
    def _():
        pl.semaphore_wait(barrier, n - 1 - me)
        rim_copy().start()

    kv_each(me, True, lambda copy: copy.start())

    for copy in in_copies[4:]:
        copy.wait()
    spread = (iota((groups, chans), 1) // GSIZE == iota((groups, chans), 0)).astype(F32)
    spread = spread.astype(BF16)
    mixed[...] = jnp.zeros(mixed.shape, F32)
    for j in range(3):
        mixed[EDGE * j:EDGE * j + reach + 1, :] = taps[j]
    mixed[3 * EDGE:, :] = rate[...]
    whole = mixed[...]
    high, rest = split_f32(whole)
    middle, rest = split_f32(rest)
    count = 3 * EDGE + modes
    spread_out = dot(jnp.concatenate([high, middle, rest], axis=0).astype(BF16), spread)
    spread_out = (spread_out[2 * count:] + spread_out[count:2 * count]) + spread_out[:count]
    for j in range(3):
        tapx[j] = spread_out[EDGE * j:EDGE * (j + 1)]
    rate_nc = spread_out[3 * EDGE:]
    step_decay = jnp.exp(rate_nc * (-float(rows)))

    for j in range(3):
        for q in range(tiles):
            ext[j * tiles + q, EDGE:, :] = xs[j, :, q * LANES:(q + 1) * LANES].astype(F32)

    def filtered(j, q, low, high):
        total = None
        for k in range(reach + 1):
            term = (tapx[j, k:k + 1, q * LANES:(q + 1) * LANES]
                    * ext[j * tiles + q, pl.ds(EDGE - k + low, high - low), :])
            total = term if total is None else total + term
        return total

    def fill_gated(low, high):
        for q in range(tiles):
            gated[low:high, q * LANES:(q + 1) * LANES] = (
                filtered(1, q, low, high) * filtered(2, q, low, high)).astype(BF16)

    fill_gated(HEAD_ROWS, rows)

    lane = iota((modes, LANES), 1).astype(F32)
    rate_v = rate[...]
    for g in range(groups):
        rate_b = jnp.broadcast_to(rate_v[:, g:g + 1], (modes, LANES))
        fall = jnp.exp(rate_b * (lane - (rows - 1.0)))
        q, gg = g // per, g % per
        falls[q, gg * modes:(gg + 1) * modes, :] = fall
        decay[q, gg * modes:(gg + 1) * modes, :] = fall.astype(BF16)

    @pl.when(me > 0)
    def _():
        rim_copy().wait_recv()
        edge = rim_rx[...].astype(F32)
        for q in range(tiles):
            cut = slice(q * LANES, (q + 1) * LANES)
            ext[tiles + q, :EDGE, :] = edge[:EDGE, cut]
            ext[2 * tiles + q, :EDGE, :] = edge[EDGE:, cut]
            place, row = (q, 0) if q < tiles // 2 else (q - tiles // 2, EDGE)
            ext[q, :EDGE, :] = edge[row:row + EDGE, chans + place * LANES:chans + (place + 1) * LANES]

    @pl.when(me == 0)
    def _():
        ext[:, :EDGE, :] = jnp.zeros((3 * tiles, EDGE, LANES), F32)

    fill_gated(0, HEAD_ROWS)

    pick = iota((modes, LANES), 1) // GSIZE
    for q in range(tiles):
        cut = slice(q * LANES, (q + 1) * LANES)
        full = dot(decay[q], gated[:, cut])
        state = jnp.zeros((modes, LANES), F32)
        for gg in range(per):
            state = jnp.where(pick == gg, full[gg * modes:(gg + 1) * modes], state)
        st_tx[:, cut] = state.astype(BF16)

    for d in range(1, n):
        @pl.when(me + d < n)
        def _():
            st_copy(d).start()

    half_rows = rows // 2
    causal = iota((half_rows, LANES), 1) <= iota((half_rows, LANES), 0) + half_rows
    residue_v = residue[...]
    for q in range(tiles):
        turned = []
        for gg in range(per):
            g = q * per + gg
            rate_b = jnp.broadcast_to(rate_v[:, g:g + 1], (modes, LANES))
            residue_b = jnp.broadcast_to(residue_v[:, g:g + 1], (modes, LANES))
            turned.append(residue_b * jnp.exp(rate_b * (-1.0 - lane)))
            fall = falls[q, gg * modes:(gg + 1) * modes, :]
            table = jnp.sum(residue_b * fall, axis=0, keepdims=True)
            rolled = pltpu.roll(
                jnp.broadcast_to(table, (half_rows, LANES)), half_rows + 1, 1,
                stride=1, stride_axis=0)
            toep[q, :, gg * LANES:(gg + 1) * LANES] = jnp.where(causal, rolled, 0.0).astype(BF16)
        coeff[q] = jnp.transpose(jnp.concatenate(turned, axis=0)).astype(BF16)

    def forward(k, carry):
        source = me - 2 * k
        kv_arrival(0, source).wait_recv()
        kv_arrival(1, source).wait_recv()
        kv_each(source, False, lambda copy: copy.start())
        return carry

    @pl.when(me < n - 1)
    def _():
        lax.fori_loop(1, me // 2 + 1, forward, 0)

    picks = [(iota((1, 2 * LANES), 1) % LANES // GSIZE == gg).astype(F32).astype(BF16)
             for gg in range(per)]
    blank = jnp.zeros((half_rows, LANES), BF16)
    for q in range(tiles):
        cut = slice(q * LANES, (q + 1) * LANES)
        own = gated[:, cut]
        moved = jnp.concatenate([blank, own[:half_rows]], axis=0)
        pair = jnp.concatenate([moved, own], axis=1)
        parts = jnp.concatenate([pair * picks[gg] for gg in range(per)], axis=0)
        near = dot(toep[q], parts)
        near = jnp.concatenate([near[:, :LANES], near[:, LANES:]], axis=0)
        longt[:, cut] = near + skip[cut].reshape(1, LANES) * own.astype(F32)
        gate[:, cut] = filtered(0, q, 0, rows)

    scale = math.log2(math.e) / math.sqrt(LANES)
    for copy in in_copies[1:4]:
        copy.wait()
    ones = jnp.ones((HEAD_ROWS, rows), BF16)
    wide = heads * rows
    last = LANES + EDGE

    def values_of(source):
        turned = jnp.transpose(kv[source, 1].astype(F32)).astype(BF16)
        return jnp.concatenate([turned, ones], axis=0)

    own_value = values_of(me)
    for c in range(wide // chunk):
        cut = slice(c * chunk, (c + 1) * chunk)
        seen = (c + 1) * chunk // heads
        scores = dot_nt(kv[me, 0, :seen, :], qv[cut, :])
        target = (iota((seen, chunk), 1) + c * chunk) // heads
        scores = jnp.where(iota((seen, chunk), 0) <= target, scores, -1e30)
        largest = jnp.max(scores, axis=0, keepdims=True)
        weights = jnp.exp2((scores - largest) * scale).astype(BF16)
        big[:, cut] = jnp.broadcast_to(largest, (EDGE, chunk))
        acc[:, cut] = dot(own_value[:, :seen], weights)[:last]

    def far_block(d, carry):
        source = me - d

        @pl.when((lax.rem(d, 2) == 1) | (me == n - 1))
        def _():
            kv_arrival(0, source).wait_recv()
            kv_arrival(1, source).wait_recv()

        value = values_of(source)
        for c in range(wide // chunk):
            cut = slice(c * chunk, (c + 1) * chunk)
            scores = dot_nt(kv[source, 0], qv[cut, :])
            before = big[:1, cut]
            largest = jnp.maximum(before, jnp.max(scores, axis=0, keepdims=True))
            weights = jnp.exp2((scores - largest) * scale).astype(BF16)
            fix = jnp.exp2((before - largest) * scale)
            big[:, cut] = jnp.broadcast_to(largest, (EDGE, chunk))
            acc[:, cut] = acc[:, cut] * fix + dot(value, weights)[:last]
        return carry

    middle_block = jnp.maximum(me, jnp.minimum(me + 1, 2))
    lax.fori_loop(1, middle_block, far_block, 0)

    def gather_state(source, state):
        st_arrival(source).wait_recv()
        return state * step_decay + st_rx[source].astype(F32)

    state = lax.fori_loop(0, me, gather_state, jnp.zeros((modes, chans), F32))
    for q in range(tiles):
        cut = slice(q * LANES, (q + 1) * LANES)
        block = jnp.concatenate(
            [jnp.where(pick == gg, state[:, cut], 0.0) for gg in range(per)], axis=0)
        far = dot(coeff[q], block.astype(BF16))
        hy_v[:, cut] = (gate[:, cut] * (longt[:, cut] + far)).astype(BF16)

    lax.fori_loop(middle_block, me + 1, far_block, 0)

    for c in range(wide // LANES):
        cut = slice(c * LANES, (c + 1) * LANES)
        ratio = acc[:LANES, cut] * (1.0 / acc[LANES:LANES + 1, cut])
        at_v[cut, :] = jnp.transpose(ratio).astype(BF16)

    @pl.when(me < n - 1)
    def _():
        rim_copy().wait_send()

    for d in range(1, n):
        @pl.when(me + d < n)
        def _():
            st_copy(d).wait_send()

    kv_each(me, True, lambda copy: copy.wait_send())

    def forwarded(k, carry):
        kv_each(me - 2 * k, False, lambda copy: copy.wait_send())
        return carry

    lax.fori_loop(1, me // 2 + 1, forwarded, 0)


def leave(hy_v, at_v, hy_out, at_out, sem):
    copies = [pltpu.make_async_copy(hy_v, hy_out, sem.at[0]),
              pltpu.make_async_copy(at_v, at_out, sem.at[1])]
    for copy in copies:
        copy.start()
    for copy in copies:
        copy.wait()


def body(n, streams, short_taps, modal_residue, modal_rate, skip_gain, queries, keys, values):
    rows, _, chans = streams.shape
    heads, size = queries.shape[1], queries.shape[2]
    modes, groups = modal_rate.shape
    tiles = chans // LANES
    per = LANES // GSIZE
    wide = heads * rows
    chunk = min(256, wide)
    reach = short_taps.shape[0]
    vmem, hbm = pl.BlockSpec(memory_space=pltpu.VMEM), pl.BlockSpec(memory_space=pltpu.HBM)
    dma = pltpu.SemaphoreType.DMA
    hyena, attn = pl.pallas_call(
        functools.partial(kernel, n, heads, chunk),
        out_shape=(jax.ShapeDtypeStruct((rows, chans), BF16),
                   jax.ShapeDtypeStruct((wide, size), BF16)),
        in_specs=[hbm] * 8,
        out_specs=(vmem, vmem),
        scratch_shapes=[
            pltpu.VMEM((3, reach, groups), F32),
            pltpu.VMEM((modes, groups), F32),
            pltpu.VMEM((modes, groups), F32),
            pltpu.VMEM((chans,), F32),
            pltpu.VMEM((3, rows, chans), BF16),
            pltpu.VMEM((wide, size), BF16),
            pltpu.VMEM((n, 2, rows, size), BF16),
            pltpu.VMEM((2 * EDGE, chans + chans // 2), BF16),
            pltpu.VMEM((2 * EDGE, chans + chans // 2), BF16),
            pltpu.VMEM((3 * tiles, rows + EDGE, LANES), F32),
            pltpu.VMEM((rows, chans), BF16),
            pltpu.VMEM((3 * EDGE + modes, groups), F32),
            pltpu.VMEM((3, EDGE, chans), F32),
            pltpu.VMEM((tiles, LANES, LANES), F32),
            pltpu.VMEM((tiles, LANES, LANES), BF16),
            pltpu.VMEM((tiles, LANES, LANES), BF16),
            pltpu.VMEM((tiles, rows // 2, per * LANES), BF16),
            pltpu.VMEM((rows, chans), F32),
            pltpu.VMEM((rows, chans), F32),
            pltpu.VMEM((modes, chans), BF16),
            pltpu.VMEM((n, modes, chans), BF16),
            pltpu.VMEM((size + EDGE, wide), F32),
            pltpu.VMEM((EDGE, wide), F32),
            dma((8,)), dma((n, 2, 2)), dma((n, 2)),
            dma, dma, dma((n,)), dma((n,)),
        ],
        compiler_params=pltpu.CompilerParams(
            collective_id=0, has_side_effects=True, vmem_limit_bytes=40 * 1024 * 1024),
        name="mixers",
    )(*[pltpu.with_memory_space_constraint(x, pltpu.HBM) for x in (
        jnp.transpose(streams, (1, 0, 2)),
        jnp.transpose(short_taps, (1, 0, 2)),
        modal_residue,
        modal_rate,
        skip_gain,
        queries.reshape(wide, size),
        keys.reshape(rows, size),
        values.reshape(rows, size),
    )])
    hyena, attn = pl.pallas_call(
        leave,
        out_shape=(jax.ShapeDtypeStruct((rows, chans), BF16),
                   jax.ShapeDtypeStruct((wide, size), BF16)),
        in_specs=[vmem, vmem],
        out_specs=(hbm, hbm),
        scratch_shapes=[dma((2,))],
        compiler_params=pltpu.CompilerParams(vmem_limit_bytes=2 * 1024 * 1024),
        name="leave",
    )(hyena, attn)
    return hyena, attn.reshape(rows, heads, size)


def solution(mesh):
    in_specs = (
        P(("dp", "ctx"), None, "mp"),
        P(None, None, "mp"),
        P(None, "mp"),
        P(None, "mp"),
        P("mp"),
        P(("dp", "ctx"), "mp", None),
        P(("dp", "ctx"), "mp", None),
        P(("dp", "ctx"), "mp", None),
    )
    out_specs = (P(("dp", "ctx"), "mp"), P(("dp", "ctx"), "mp", None))
    return jax.shard_map(functools.partial(body, mesh.shape["ctx"]), mesh=mesh,
                         in_specs=in_specs, out_specs=out_specs, check_vma=False)
```

```python
import functools
import math

import jax
import jax.numpy as jnp
from jax import lax
from jax.experimental import pallas as pl
from jax.experimental.pallas import tpu as pltpu
from jax.sharding import PartitionSpec as P

GSIZE = 16
LANES = 128
EDGE = 8
HEAD_ROWS = 16
MESH = pl.DeviceIdType.MESH
BF16 = jnp.bfloat16
F32 = jnp.float32


def iota(shape, axis):
    return lax.broadcasted_iota(jnp.int32, shape, axis)


def dot(a, b):
    return jnp.dot(a, b, preferred_element_type=F32)


def dot_nt(a, b):
    return lax.dot_general(a, b, (((1,), (1,)), ((), ())), preferred_element_type=F32)


def split_f32(value):
    high = value.astype(BF16).astype(F32)
    return high, value - high


def kernel(
    n, heads, chunk,
    streams, taps_in, residue_in, rate_in, skip_in, q_in, k_in, v_in,
    hy_v, at_v,
    taps, residue, rate, skip,
    xs, qv, kv, rim_tx, rim_rx, ext, gated, mixed, tapx, falls, decay, coeff, toep, longt, gate,
    st_tx, st_rx, run_p, run_e, acc, big, fixes, wts,
    in_sem, kv_send, kv_recv, rim_send, rim_recv, st_send, st_recv,
):
    me = lax.axis_index("ctx")
    rows, chans = xs.shape[1], xs.shape[2]
    modes, groups = rate.shape
    reach = taps.shape[1] - 1
    tiles = chans // LANES
    per = LANES // GSIZE
    half = chans // 2

    in_copies = [
        pltpu.make_async_copy(streams, xs, in_sem.at[0]),
        pltpu.make_async_copy(k_in, kv.at[me, 0], in_sem.at[1]),
        pltpu.make_async_copy(v_in, kv.at[me, 1], in_sem.at[2]),
        pltpu.make_async_copy(q_in, qv, in_sem.at[3]),
        pltpu.make_async_copy(rate_in, rate, in_sem.at[4]),
        pltpu.make_async_copy(residue_in, residue, in_sem.at[5]),
        pltpu.make_async_copy(taps_in, taps, in_sem.at[6]),
        pltpu.make_async_copy(skip_in, skip, in_sem.at[7]),
    ]
    for copy in in_copies:
        copy.start()

    barrier = pltpu.get_barrier_semaphore()
    for d in range(1, n):
        @pl.when(me >= d)
        def _():
            pl.semaphore_signal(barrier, inc=1, device_id={"ctx": me - d}, device_id_type=MESH)

    def kv_copy(part, source, d, own=False):
        src = (k_in if part == 0 else v_in) if own else kv.at[source, part]
        return pltpu.make_async_remote_copy(
            src_ref=src, dst_ref=kv.at[source, part], send_sem=kv_send.at[source, d - 1, part],
            recv_sem=kv_recv.at[source, part], device_id={"ctx": me + d}, device_id_type=MESH)

    def kv_each(source, own, act, parts=(0, 1)):
        for d in (2, 1):
            @pl.when(me + d < n)
            def _():
                for part in parts:
                    act(kv_copy(part, source, d, own))

    def kv_arrival(part, source):
        return pltpu.make_async_remote_copy(
            src_ref=kv.at[source, part], dst_ref=kv.at[source, part], send_sem=kv_send.at[source, 0, part],
            recv_sem=kv_recv.at[source, part], device_id={"ctx": source}, device_id_type=MESH)

    steps = (n - 1).bit_length()

    def st_copy(k):
        return pltpu.make_async_remote_copy(
            src_ref=st_tx.at[k], dst_ref=st_rx.at[k], send_sem=st_send.at[k],
            recv_sem=st_recv.at[k], device_id={"ctx": lax.rem(me + 2 ** k, n)},
            device_id_type=MESH)

    def st_out(k):
        st_tx[k] = run_p[...].astype(BF16)

        @pl.when(me + 2 ** k < n)
        def _():
            st_copy(k).start()

    def st_in(k):
        @pl.when(me >= 2 ** k)
        def _():
            st_copy(k).wait_recv()
            got = st_rx[k].astype(F32)
            fall = -float(rows) * rate_nc
            run_e[...] += got if k == 0 else got * jnp.exp(fall * (2 ** k - 1.0))
            if k + 1 < steps:
                run_p[...] += got * jnp.exp(fall * float(2 ** k))

    def rim_copy():
        return pltpu.make_async_remote_copy(
            src_ref=rim_tx, dst_ref=rim_rx, send_sem=rim_send, recv_sem=rim_recv,
            device_id={"ctx": lax.rem(me + 1, n)}, device_id_type=MESH)

    in_copies[0].wait()
    tail = xs[:, rows - HEAD_ROWS:, :].astype(F32)[:, HEAD_ROWS - EDGE:, :]
    rim_tx[:, :chans] = jnp.concatenate([tail[1], tail[2]], axis=0).astype(BF16)
    rim_tx[:, chans:] = jnp.concatenate([tail[0, :, :half], tail[0, :, half:]], axis=0).astype(BF16)

    @pl.when(me < n - 1)
    def _():
        pl.semaphore_wait(barrier, n - 1 - me)
        rim_copy().start()

    kv_each(me, True, lambda copy: copy.start())

    for copy in in_copies[4:]:
        copy.wait()
    spread = (iota((groups, chans), 1) // GSIZE == iota((groups, chans), 0)).astype(F32)
    spread = spread.astype(BF16)
    mixed[...] = jnp.zeros(mixed.shape, F32)
    for j in range(3):
        mixed[EDGE * j:EDGE * j + reach + 1, :] = taps[j]
    mixed[3 * EDGE:, :] = rate[...]
    whole = mixed[...]
    high, rest = split_f32(whole)
    middle, rest = split_f32(rest)
    count = 3 * EDGE + modes
    spread_out = dot(jnp.concatenate([high, middle, rest], axis=0).astype(BF16), spread)
    spread_out = (spread_out[2 * count:] + spread_out[count:2 * count]) + spread_out[:count]
    for j in range(3):
        tapx[j] = spread_out[EDGE * j:EDGE * (j + 1)]
    rate_nc = spread_out[3 * EDGE:]

    for j in range(3):
        for q in range(tiles):
            ext[j * tiles + q, EDGE:, :] = xs[j, :, q * LANES:(q + 1) * LANES].astype(F32)

    def filtered(j, q, low, high):
        total = None
        for k in range(reach + 1):
            term = (tapx[j, k:k + 1, q * LANES:(q + 1) * LANES]
                    * ext[j * tiles + q, pl.ds(EDGE - k + low, high - low), :])
            total = term if total is None else total + term
        return total

    def fill_gated(low, high):
        for q in range(tiles):
            gated[low:high, q * LANES:(q + 1) * LANES] = (
                filtered(1, q, low, high) * filtered(2, q, low, high)).astype(BF16)

    fill_gated(HEAD_ROWS, rows)

    lane = iota((modes, LANES), 1).astype(F32)
    rate_v = rate[...]
    for g in range(groups):
        rate_b = jnp.broadcast_to(rate_v[:, g:g + 1], (modes, LANES))
        fall = jnp.exp(rate_b * (lane - (rows - 1.0)))
        q, gg = g // per, g % per
        falls[q, gg * modes:(gg + 1) * modes, :] = fall
        decay[q, gg * modes:(gg + 1) * modes, :] = fall.astype(BF16)

    @pl.when(me > 0)
    def _():
        rim_copy().wait_recv()
        edge = rim_rx[...].astype(F32)
        for q in range(tiles):
            cut = slice(q * LANES, (q + 1) * LANES)
            ext[tiles + q, :EDGE, :] = edge[:EDGE, cut]
            ext[2 * tiles + q, :EDGE, :] = edge[EDGE:, cut]
            place, row = (q, 0) if q < tiles // 2 else (q - tiles // 2, EDGE)
            ext[q, :EDGE, :] = edge[row:row + EDGE, chans + place * LANES:chans + (place + 1) * LANES]

    @pl.when(me == 0)
    def _():
        ext[:, :EDGE, :] = jnp.zeros((3 * tiles, EDGE, LANES), F32)

    fill_gated(0, HEAD_ROWS)

    pick = iota((modes, LANES), 1) // GSIZE
    for q in range(tiles):
        cut = slice(q * LANES, (q + 1) * LANES)
        full = dot(decay[q], gated[:, cut])
        state = jnp.zeros((modes, LANES), F32)
        for gg in range(per):
            state = jnp.where(pick == gg, full[gg * modes:(gg + 1) * modes], state)
        run_p[:, cut] = state
    run_e[...] = jnp.zeros(run_e.shape, F32)
    st_out(0)

    half_rows = rows // 2
    causal = iota((half_rows, LANES), 1) <= iota((half_rows, LANES), 0) + half_rows
    residue_v = residue[...]
    for q in range(tiles):
        turned = []
        for gg in range(per):
            g = q * per + gg
            rate_b = jnp.broadcast_to(rate_v[:, g:g + 1], (modes, LANES))
            residue_b = jnp.broadcast_to(residue_v[:, g:g + 1], (modes, LANES))
            turned.append(residue_b * jnp.exp(rate_b * (-1.0 - lane)))
            fall = falls[q, gg * modes:(gg + 1) * modes, :]
            table = jnp.sum(residue_b * fall, axis=0, keepdims=True)
            rolled = pltpu.roll(
                jnp.broadcast_to(table, (half_rows, LANES)), half_rows + 1, 1,
                stride=1, stride_axis=0)
            toep[q, :, gg * LANES:(gg + 1) * LANES] = jnp.where(causal, rolled, 0.0).astype(BF16)
        coeff[q] = jnp.transpose(jnp.concatenate(turned, axis=0)).astype(BF16)

    def forward(k, carry):
        source = me - 2 * k
        for part in range(2):
            kv_arrival(part, source).wait_recv()
            kv_each(source, False, lambda copy: copy.start(), (part,))
        return carry

    @pl.when(me < n - 1)
    def _():
        lax.fori_loop(1, me // 2 + 1, forward, 0)

    picks = [(iota((1, 2 * LANES), 1) % LANES // GSIZE == gg).astype(F32).astype(BF16)
             for gg in range(per)]
    blank = jnp.zeros((half_rows, LANES), BF16)
    for q in range(tiles):
        cut = slice(q * LANES, (q + 1) * LANES)
        own = gated[:, cut]
        moved = jnp.concatenate([blank, own[:half_rows]], axis=0)
        pair = jnp.concatenate([moved, own], axis=1)
        parts = jnp.concatenate([pair * picks[gg] for gg in range(per)], axis=0)
        near = dot(toep[q], parts)
        near = jnp.concatenate([near[:, :LANES], near[:, LANES:]], axis=0)
        longt[:, cut] = near + skip[cut].reshape(1, LANES) * own.astype(F32)
        gate[:, cut] = filtered(0, q, 0, rows)

    for k in range(steps - 1):
        st_in(k)
        st_out(k + 1)

    scale = math.log2(math.e) / math.sqrt(LANES)
    for copy in in_copies[1:4]:
        copy.wait()
    ones = jnp.ones((HEAD_ROWS, rows), BF16)
    wide = heads * rows
    last = LANES + EDGE

    def values_of(source):
        turned = jnp.transpose(kv[source, 1].astype(F32)).astype(BF16)
        return jnp.concatenate([turned, ones], axis=0)

    own_value = values_of(me)
    for c in range(wide // chunk):
        cut = slice(c * chunk, (c + 1) * chunk)
        seen = (c + 1) * chunk // heads
        scores = dot_nt(kv[me, 0, :seen, :], qv[cut, :])
        target = (iota((seen, chunk), 1) + c * chunk) // heads
        scores = jnp.where(iota((seen, chunk), 0) <= target, scores, -1e30)
        largest = jnp.max(scores, axis=0, keepdims=True)
        weights = jnp.exp2((scores - largest) * scale).astype(BF16)
        big[:, cut] = jnp.broadcast_to(largest, (EDGE, chunk))
        acc[:, cut] = dot(own_value[:, :seen], weights)[:last]

    def weigh(source, waits):
        @pl.when(waits)
        def _():
            kv_arrival(0, source).wait_recv()

        for c in range(wide // chunk):
            cut = slice(c * chunk, (c + 1) * chunk)
            scores = dot_nt(kv[source, 0], qv[cut, :])
            before = big[:1, cut]
            largest = jnp.maximum(before, jnp.max(scores, axis=0, keepdims=True))
            wts[:, cut] = jnp.exp2((scores - largest) * scale).astype(BF16)
            fix = jnp.exp2((before - largest) * scale)
            big[:, cut] = jnp.broadcast_to(largest, (EDGE, chunk))
            fixes[:, cut] = jnp.broadcast_to(fix, (EDGE, chunk))

        @pl.when(waits)
        def _():
            kv_arrival(1, source).wait_recv()

    def finish(c, total):
        for part in range(chunk // LANES):
            cut = slice(part * LANES, (part + 1) * LANES)
            ratio = total[:LANES, cut] * (1.0 / total[LANES:LANES + 1, cut])
            low = c * chunk + part * LANES
            at_v[low:low + LANES, :] = jnp.transpose(ratio).astype(BF16)

    def far_block(d, carry):
        source = me - d
        weigh(source, (lax.rem(d, 2) == 1) | (me == n - 1))
        value = values_of(source)
        for c in range(wide // chunk):
            cut = slice(c * chunk, (c + 1) * chunk)
            acc[:, cut] = acc[:, cut] * fixes[:1, cut] + dot(value, wts[:, cut])[:last]
        return carry

    lax.fori_loop(1, me, far_block, 0)

    st_in(steps - 1)
    for q in range(tiles):
        cut = slice(q * LANES, (q + 1) * LANES)
        block = jnp.concatenate(
            [jnp.where(pick == gg, run_e[:, cut], 0.0) for gg in range(per)], axis=0)
        far = dot(coeff[q], block.astype(BF16))
        hy_v[:, cut] = (gate[:, cut] * (longt[:, cut] + far)).astype(BF16)

    @pl.when(me > 0)
    def _():
        weigh(0, (lax.rem(me, 2) == 1) | (me == n - 1))
        value = values_of(0)
        for c in range(wide // chunk):
            cut = slice(c * chunk, (c + 1) * chunk)
            finish(c, acc[:, cut] * fixes[:1, cut] + dot(value, wts[:, cut])[:last])

    @pl.when(me == 0)
    def _():
        for c in range(wide // chunk):
            finish(c, acc[:, c * chunk:(c + 1) * chunk])

    @pl.when(me < n - 1)
    def _():
        rim_copy().wait_send()

    for k in range(steps):
        @pl.when(me + 2 ** k < n)
        def _():
            st_copy(k).wait_send()

    kv_each(me, True, lambda copy: copy.wait_send())

    def forwarded(k, carry):
        kv_each(me - 2 * k, False, lambda copy: copy.wait_send())
        return carry

    lax.fori_loop(1, me // 2 + 1, forwarded, 0)


def leave(hy_v, at_v, hy_out, at_out, sem):
    copies = [pltpu.make_async_copy(hy_v, hy_out, sem.at[0]),
              pltpu.make_async_copy(at_v, at_out, sem.at[1])]
    for copy in copies:
        copy.start()
    for copy in copies:
        copy.wait()


def body(n, streams, short_taps, modal_residue, modal_rate, skip_gain, queries, keys, values):
    rows, _, chans = streams.shape
    heads, size = queries.shape[1], queries.shape[2]
    modes, groups = modal_rate.shape
    tiles = chans // LANES
    per = LANES // GSIZE
    wide = heads * rows
    chunk = min(256, wide)
    reach = short_taps.shape[0]
    steps = (n - 1).bit_length()
    vmem, hbm = pl.BlockSpec(memory_space=pltpu.VMEM), pl.BlockSpec(memory_space=pltpu.HBM)
    dma = pltpu.SemaphoreType.DMA
    hyena, attn = pl.pallas_call(
        functools.partial(kernel, n, heads, chunk),
        out_shape=(jax.ShapeDtypeStruct((rows, chans), BF16),
                   jax.ShapeDtypeStruct((wide, size), BF16)),
        in_specs=[hbm] * 8,
        out_specs=(vmem, vmem),
        scratch_shapes=[
            pltpu.VMEM((3, reach, groups), F32),
            pltpu.VMEM((modes, groups), F32),
            pltpu.VMEM((modes, groups), F32),
            pltpu.VMEM((chans,), F32),
            pltpu.VMEM((3, rows, chans), BF16),
            pltpu.VMEM((wide, size), BF16),
            pltpu.VMEM((n, 2, rows, size), BF16),
            pltpu.VMEM((2 * EDGE, chans + chans // 2), BF16),
            pltpu.VMEM((2 * EDGE, chans + chans // 2), BF16),
            pltpu.VMEM((3 * tiles, rows + EDGE, LANES), F32),
            pltpu.VMEM((rows, chans), BF16),
            pltpu.VMEM((3 * EDGE + modes, groups), F32),
            pltpu.VMEM((3, EDGE, chans), F32),
            pltpu.VMEM((tiles, LANES, LANES), F32),
            pltpu.VMEM((tiles, LANES, LANES), BF16),
            pltpu.VMEM((tiles, LANES, LANES), BF16),
            pltpu.VMEM((tiles, rows // 2, per * LANES), BF16),
            pltpu.VMEM((rows, chans), F32),
            pltpu.VMEM((rows, chans), F32),
            pltpu.VMEM((steps, modes, chans), BF16),
            pltpu.VMEM((steps, modes, chans), BF16),
            pltpu.VMEM((modes, chans), F32),
            pltpu.VMEM((modes, chans), F32),
            pltpu.VMEM((size + EDGE, wide), F32),
            pltpu.VMEM((EDGE, wide), F32),
            pltpu.VMEM((EDGE, wide), F32),
            pltpu.VMEM((rows, wide), BF16),
            dma((8,)), dma((n, 2, 2)), dma((n, 2)),
            dma, dma, dma((steps,)), dma((steps,)),
        ],
        compiler_params=pltpu.CompilerParams(
            collective_id=0, has_side_effects=True, vmem_limit_bytes=40 * 1024 * 1024),
        name="mixers",
    )(*[pltpu.with_memory_space_constraint(x, pltpu.HBM) for x in (
        jnp.transpose(streams, (1, 0, 2)),
        jnp.transpose(short_taps, (1, 0, 2)),
        modal_residue,
        modal_rate,
        skip_gain,
        queries.reshape(wide, size),
        keys.reshape(rows, size),
        values.reshape(rows, size),
    )])
    hyena, attn = pl.pallas_call(
        leave,
        out_shape=(jax.ShapeDtypeStruct((rows, chans), BF16),
                   jax.ShapeDtypeStruct((wide, size), BF16)),
        in_specs=[vmem, vmem],
        out_specs=(hbm, hbm),
        scratch_shapes=[dma((2,))],
        compiler_params=pltpu.CompilerParams(vmem_limit_bytes=2 * 1024 * 1024),
        name="leave",
    )(hyena, attn)
    return hyena, attn.reshape(rows, heads, size)


def solution(mesh):
    in_specs = (
        P(("dp", "ctx"), None, "mp"),
        P(None, None, "mp"),
        P(None, "mp"),
        P(None, "mp"),
        P("mp"),
        P(("dp", "ctx"), "mp", None),
        P(("dp", "ctx"), "mp", None),
        P(("dp", "ctx"), "mp", None),
    )
    out_specs = (P(("dp", "ctx"), "mp"), P(("dp", "ctx"), "mp", None))
    return jax.shard_map(functools.partial(body, mesh.shape["ctx"]), mesh=mesh,
                         in_specs=in_specs, out_specs=out_specs, check_vma=False)
```

```python
import functools
import math

import jax
import jax.numpy as jnp
from jax import lax
from jax.experimental import pallas as pl
from jax.experimental.pallas import tpu as pltpu
from jax.sharding import PartitionSpec as P

GSIZE = 16
LANES = 128
EDGE = 8
HEAD_ROWS = 16
MESH = pl.DeviceIdType.MESH
BF16 = jnp.bfloat16
F32 = jnp.float32


def iota(shape, axis):
    return lax.broadcasted_iota(jnp.int32, shape, axis)


def dot(a, b):
    return jnp.dot(a, b, preferred_element_type=F32)


def dot_nt(a, b):
    return lax.dot_general(a, b, (((1,), (1,)), ((), ())), preferred_element_type=F32)


def split_f32(value):
    high = value.astype(BF16).astype(F32)
    return high, value - high


def kernel(
    n, heads, chunk,
    streams, taps_in, residue_in, rate_in, skip_in, q_in, k_in, v_in,
    hy_v, at_v,
    taps, residue, rate, skip,
    xs, qv, kv, rim_tx, rim_rx, ext, gated, mixed, rates, residues, skips, tapx, falls, decay, coeff, longt, gate,
    st_tx, st_rx, acc, big,
    in_sem, kv_send, kv_recv, rim_send, rim_recv, st_send, st_recv,
):
    me = lax.axis_index("ctx")
    rows, chans = xs.shape[1], xs.shape[2]
    modes, groups = rate.shape
    reach = taps.shape[1] - 1
    tiles = chans // LANES
    per = LANES // GSIZE
    half = chans // 2

    in_copies = [
        pltpu.make_async_copy(streams, xs, in_sem.at[0]),
        pltpu.make_async_copy(k_in, kv.at[me, 0], in_sem.at[1]),
        pltpu.make_async_copy(v_in, kv.at[me, 1], in_sem.at[2]),
        pltpu.make_async_copy(q_in, qv, in_sem.at[3]),
        pltpu.make_async_copy(rate_in, rate, in_sem.at[4]),
        pltpu.make_async_copy(residue_in, residue, in_sem.at[5]),
        pltpu.make_async_copy(taps_in, taps, in_sem.at[6]),
        pltpu.make_async_copy(skip_in, skip, in_sem.at[7]),
    ]
    for copy in in_copies:
        copy.start()

    barrier = pltpu.get_barrier_semaphore()
    for d in range(1, n):
        @pl.when(me >= d)
        def _():
            pl.semaphore_signal(barrier, inc=1, device_id={"ctx": me - d}, device_id_type=MESH)

    def kv_copy(part, source, d, own=False):
        src = (k_in if part == 0 else v_in) if own else kv.at[source, part]
        return pltpu.make_async_remote_copy(
            src_ref=src, dst_ref=kv.at[source, part], send_sem=kv_send.at[source, d - 1, part],
            recv_sem=kv_recv.at[source, part], device_id={"ctx": me + d}, device_id_type=MESH)

    def kv_each(source, own, act):
        for d in (2, 1):
            @pl.when(me + d < n)
            def _():
                act(kv_copy(0, source, d, own))
                act(kv_copy(1, source, d, own))

    def kv_arrival(part, source):
        return pltpu.make_async_remote_copy(
            src_ref=kv.at[source, part], dst_ref=kv.at[source, part], send_sem=kv_send.at[source, 0, part],
            recv_sem=kv_recv.at[source, part], device_id={"ctx": source}, device_id_type=MESH)

    def st_copy(d):
        return pltpu.make_async_remote_copy(
            src_ref=st_tx, dst_ref=st_rx.at[me], send_sem=st_send.at[d],
            recv_sem=st_recv.at[me], device_id={"ctx": me + d}, device_id_type=MESH)

    def st_arrival(source):
        return pltpu.make_async_remote_copy(
            src_ref=st_tx, dst_ref=st_rx.at[source], send_sem=st_send.at[0],
            recv_sem=st_recv.at[source], device_id={"ctx": source}, device_id_type=MESH)

    def rim_copy():
        return pltpu.make_async_remote_copy(
            src_ref=rim_tx, dst_ref=rim_rx, send_sem=rim_send, recv_sem=rim_recv,
            device_id={"ctx": lax.rem(me + 1, n)}, device_id_type=MESH)

    in_copies[0].wait()
    tail = xs[:, rows - HEAD_ROWS:, :].astype(F32)[:, HEAD_ROWS - EDGE:, :]
    rim_tx[:, :chans] = jnp.concatenate([tail[1], tail[2]], axis=0).astype(BF16)
    rim_tx[:, chans:] = jnp.concatenate([tail[0, :, :half], tail[0, :, half:]], axis=0).astype(BF16)

    @pl.when(me < n - 1)
    def _():
        pl.semaphore_wait(barrier, n - 1 - me)
        rim_copy().start()

    kv_each(me, True, lambda copy: copy.start())

    for copy in in_copies[4:]:
        copy.wait()
    spread = (iota((groups, chans), 1) // GSIZE == iota((groups, chans), 0)).astype(F32)
    spread = spread.astype(BF16)
    mixed[...] = jnp.zeros(mixed.shape, F32)
    for j in range(3):
        mixed[EDGE * j:EDGE * j + reach + 1, :] = taps[j]
    mixed[3 * EDGE:3 * EDGE + modes, :] = rate[...]
    mixed[3 * EDGE + modes:, :] = residue[...]
    whole = mixed[...]
    high, rest = split_f32(whole)
    middle, rest = split_f32(rest)
    count = 3 * EDGE + 2 * modes
    spread_out = dot(jnp.concatenate([high, middle, rest], axis=0).astype(BF16), spread)
    spread_out = (spread_out[2 * count:] + spread_out[count:2 * count]) + spread_out[:count]
    for j in range(3):
        tapx[j] = spread_out[EDGE * j:EDGE * (j + 1)]
    rate_nc = spread_out[3 * EDGE:3 * EDGE + modes]
    rates[...] = rate_nc
    residues[...] = spread_out[3 * EDGE + modes:]
    step_decay = jnp.exp(rate_nc * (-float(rows)))

    for q in range(tiles):
        skips[:1, q * LANES:(q + 1) * LANES] = skip[q * LANES:(q + 1) * LANES].reshape(1, LANES)

    def lanes_of(q):
        if isinstance(q, int):
            return pl.ds(q * LANES, LANES)
        return pl.ds(pl.multiple_of(q * LANES, LANES), LANES)

    def filtered(j, q, low, high):
        total = None
        for k in range(reach + 1):
            term = (tapx[j, k:k + 1, lanes_of(q)]
                    * ext[j * tiles + q, pl.ds(EDGE - k + low, high - low), :])
            total = term if total is None else total + term
        return total

    def fill_gated(q, low, high):
        gated[low:high, lanes_of(q)] = (
            filtered(1, q, low, high) * filtered(2, q, low, high)).astype(BF16)

    lane = iota((modes, LANES), 1).astype(F32)

    def prepare(q, carry):
        for j in range(3):
            ext[j * tiles + q, EDGE:, :] = xs[j, :, lanes_of(q)].astype(F32)
        fill_gated(q, HEAD_ROWS, rows)
        rate_v = rates[:, lanes_of(q)]
        for gg in range(per):
            rate_b = jnp.broadcast_to(rate_v[:, gg * GSIZE:gg * GSIZE + 1], (modes, LANES))
            fall = jnp.exp(rate_b * (lane - (rows - 1.0)))
            falls[q, gg * modes:(gg + 1) * modes, :] = fall
            decay[q, gg * modes:(gg + 1) * modes, :] = fall.astype(BF16)
        return carry

    lax.fori_loop(0, tiles, prepare, 0)

    @pl.when(me > 0)
    def _():
        rim_copy().wait_recv()
        edge = rim_rx[...].astype(F32)
        for q in range(tiles):
            cut = slice(q * LANES, (q + 1) * LANES)
            ext[tiles + q, :EDGE, :] = edge[:EDGE, cut]
            ext[2 * tiles + q, :EDGE, :] = edge[EDGE:, cut]
            place, row = (q, 0) if q < tiles // 2 else (q - tiles // 2, EDGE)
            ext[q, :EDGE, :] = edge[row:row + EDGE, chans + place * LANES:chans + (place + 1) * LANES]

    @pl.when(me == 0)
    def _():
        ext[:, :EDGE, :] = jnp.zeros((3 * tiles, EDGE, LANES), F32)

    for q in range(tiles):
        fill_gated(q, 0, HEAD_ROWS)

    pick = iota((modes, LANES), 1) // GSIZE
    for q in range(tiles):
        cut = slice(q * LANES, (q + 1) * LANES)
        full = dot(decay[q], gated[:, cut])
        state = jnp.zeros((modes, LANES), F32)
        for gg in range(per):
            state = jnp.where(pick == gg, full[gg * modes:(gg + 1) * modes], state)
        st_tx[:, cut] = state.astype(BF16)

    for d in range(1, n):
        @pl.when(me + d < n)
        def _():
            st_copy(d).start()

    half_rows = rows // 2
    causal = iota((half_rows, LANES), 1) <= iota((half_rows, LANES), 0) + half_rows
    picks = [(iota((1, 2 * LANES), 1) % LANES // GSIZE == gg).astype(F32).astype(BF16)
             for gg in range(per)]
    blank = jnp.zeros((half_rows, LANES), BF16)

    def forward(k, carry):
        source = me - 2 * k
        kv_arrival(0, source).wait_recv()
        kv_arrival(1, source).wait_recv()
        kv_each(source, False, lambda copy: copy.start())
        return carry

    def near_tile(q, carry):
        @pl.when((q == tiles - 2) & (me < n - 1))
        def _():
            lax.fori_loop(1, me // 2 + 1, forward, 0)

        rate_v = rates[:, lanes_of(q)]
        residue_v = residues[:, lanes_of(q)]
        turned, blocks = [], []
        for gg in range(per):
            one = slice(gg * GSIZE, gg * GSIZE + 1)
            rate_b = jnp.broadcast_to(rate_v[:, one], (modes, LANES))
            residue_b = jnp.broadcast_to(residue_v[:, one], (modes, LANES))
            turned.append(residue_b * jnp.exp(rate_b * (-1.0 - lane)))
            fall = falls[q, gg * modes:(gg + 1) * modes, :]
            table = jnp.sum(residue_b * fall, axis=0, keepdims=True)
            rolled = pltpu.roll(
                jnp.broadcast_to(table, (half_rows, LANES)), half_rows + 1, 1,
                stride=1, stride_axis=0)
            blocks.append(jnp.where(causal, rolled, 0.0).astype(BF16))
        own = gated[:, lanes_of(q)]
        moved = jnp.concatenate([blank, own[:half_rows]], axis=0)
        pair = jnp.concatenate([moved, own], axis=1)
        parts = jnp.concatenate([pair * picks[gg] for gg in range(per)], axis=0)
        near = dot(jnp.concatenate(blocks, axis=1), parts)
        near = jnp.concatenate([near[:, :LANES], near[:, LANES:]], axis=0)
        coeff[q] = jnp.transpose(jnp.concatenate(turned, axis=0)).astype(BF16)
        gate[:, lanes_of(q)] = filtered(0, q, 0, rows)
        longt[:, lanes_of(q)] = near + skips[:1, lanes_of(q)] * own.astype(F32)
        return carry

    lax.fori_loop(0, tiles, near_tile, 0)

    scale = math.log2(math.e) / math.sqrt(LANES)
    for copy in in_copies[1:4]:
        copy.wait()
    ones = jnp.ones((HEAD_ROWS, rows), BF16)
    wide = heads * rows
    last = LANES + EDGE

    def values_of(source):
        turned = jnp.transpose(kv[source, 1].astype(F32)).astype(BF16)
        return jnp.concatenate([turned, ones], axis=0)

    own_value = values_of(me)
    for c in range(wide // chunk):
        cut = slice(c * chunk, (c + 1) * chunk)
        seen = (c + 1) * chunk // heads
        scores = dot_nt(kv[me, 0, :seen, :], qv[cut, :])
        target = (iota((seen, chunk), 1) + c * chunk) // heads
        scores = jnp.where(iota((seen, chunk), 0) <= target, scores, -1e30)
        largest = jnp.max(scores, axis=0, keepdims=True)
        weights = jnp.exp2((scores - largest) * scale).astype(BF16)
        big[:, cut] = jnp.broadcast_to(largest, (EDGE, chunk))
        acc[:, cut] = dot(own_value[:, :seen], weights)[:last]

    def far_block(d, carry):
        source = me - d

        @pl.when((lax.rem(d, 2) == 1) | (me == n - 1))
        def _():
            kv_arrival(0, source).wait_recv()
            kv_arrival(1, source).wait_recv()

        value = values_of(source)
        for c in range(wide // chunk):
            cut = slice(c * chunk, (c + 1) * chunk)
            scores = dot_nt(kv[source, 0], qv[cut, :])
            before = big[:1, cut]
            largest = jnp.maximum(before, jnp.max(scores, axis=0, keepdims=True))
            weights = jnp.exp2((scores - largest) * scale).astype(BF16)
            fix = jnp.exp2((before - largest) * scale)
            big[:, cut] = jnp.broadcast_to(largest, (EDGE, chunk))
            acc[:, cut] = acc[:, cut] * fix + dot(value, weights)[:last]
        return carry

    def gather_state(source, state):
        st_arrival(source).wait_recv()
        return state * step_decay + st_rx[source].astype(F32)

    state = lax.fori_loop(0, me, gather_state, jnp.zeros((modes, chans), F32))
    for q in range(tiles):
        cut = slice(q * LANES, (q + 1) * LANES)
        block = jnp.concatenate(
            [jnp.where(pick == gg, state[:, cut], 0.0) for gg in range(per)], axis=0)
        far = dot(coeff[q], block.astype(BF16))
        hy_v[:, cut] = (gate[:, cut] * (longt[:, cut] + far)).astype(BF16)

    lax.fori_loop(1, me + 1, far_block, 0)

    for c in range(wide // LANES):
        cut = slice(c * LANES, (c + 1) * LANES)
        ratio = acc[:LANES, cut] * (1.0 / acc[LANES:LANES + 1, cut])
        at_v[cut, :] = jnp.transpose(ratio).astype(BF16)

    @pl.when(me < n - 1)
    def _():
        rim_copy().wait_send()

    for d in range(1, n):
        @pl.when(me + d < n)
        def _():
            st_copy(d).wait_send()

    kv_each(me, True, lambda copy: copy.wait_send())

    def forwarded(k, carry):
        kv_each(me - 2 * k, False, lambda copy: copy.wait_send())
        return carry

    lax.fori_loop(1, me // 2 + 1, forwarded, 0)


def leave(hy_v, at_v, hy_out, at_out, sem):
    copies = [pltpu.make_async_copy(hy_v, hy_out, sem.at[0]),
              pltpu.make_async_copy(at_v, at_out, sem.at[1])]
    for copy in copies:
        copy.start()
    for copy in copies:
        copy.wait()


def body(n, streams, short_taps, modal_residue, modal_rate, skip_gain, queries, keys, values):
    rows, _, chans = streams.shape
    heads, size = queries.shape[1], queries.shape[2]
    modes, groups = modal_rate.shape
    tiles = chans // LANES
    per = LANES // GSIZE
    wide = heads * rows
    chunk = min(256, wide)
    reach = short_taps.shape[0]
    vmem, hbm = pl.BlockSpec(memory_space=pltpu.VMEM), pl.BlockSpec(memory_space=pltpu.HBM)
    dma = pltpu.SemaphoreType.DMA
    hyena, attn = pl.pallas_call(
        functools.partial(kernel, n, heads, chunk),
        out_shape=(jax.ShapeDtypeStruct((rows, chans), BF16),
                   jax.ShapeDtypeStruct((wide, size), BF16)),
        in_specs=[hbm] * 8,
        out_specs=(vmem, vmem),
        scratch_shapes=[
            pltpu.VMEM((3, reach, groups), F32),
            pltpu.VMEM((modes, groups), F32),
            pltpu.VMEM((modes, groups), F32),
            pltpu.VMEM((chans,), F32),
            pltpu.VMEM((3, rows, chans), BF16),
            pltpu.VMEM((wide, size), BF16),
            pltpu.VMEM((n, 2, rows, size), BF16),
            pltpu.VMEM((2 * EDGE, chans + chans // 2), BF16),
            pltpu.VMEM((2 * EDGE, chans + chans // 2), BF16),
            pltpu.VMEM((3 * tiles, rows + EDGE, LANES), F32),
            pltpu.VMEM((rows, chans), BF16),
            pltpu.VMEM((3 * EDGE + 2 * modes, groups), F32),
            pltpu.VMEM((modes, chans), F32),
            pltpu.VMEM((modes, chans), F32),
            pltpu.VMEM((EDGE, chans), F32),
            pltpu.VMEM((3, EDGE, chans), F32),
            pltpu.VMEM((tiles, LANES, LANES), F32),
            pltpu.VMEM((tiles, LANES, LANES), BF16),
            pltpu.VMEM((tiles, LANES, LANES), BF16),
            pltpu.VMEM((rows, chans), F32),
            pltpu.VMEM((rows, chans), F32),
            pltpu.VMEM((modes, chans), BF16),
            pltpu.VMEM((n, modes, chans), BF16),
            pltpu.VMEM((size + EDGE, wide), F32),
            pltpu.VMEM((EDGE, wide), F32),
            dma((8,)), dma((n, 2, 2)), dma((n, 2)),
            dma, dma, dma((n,)), dma((n,)),
        ],
        compiler_params=pltpu.CompilerParams(
            collective_id=0, has_side_effects=True, vmem_limit_bytes=40 * 1024 * 1024),
        name="mixers",
    )(*[pltpu.with_memory_space_constraint(x, pltpu.HBM) for x in (
        jnp.transpose(streams, (1, 0, 2)),
        jnp.transpose(short_taps, (1, 0, 2)),
        modal_residue,
        modal_rate,
        skip_gain,
        queries.reshape(wide, size),
        keys.reshape(rows, size),
        values.reshape(rows, size),
    )])
    hyena, attn = pl.pallas_call(
        leave,
        out_shape=(jax.ShapeDtypeStruct((rows, chans), BF16),
                   jax.ShapeDtypeStruct((wide, size), BF16)),
        in_specs=[vmem, vmem],
        out_specs=(hbm, hbm),
        scratch_shapes=[dma((2,))],
        compiler_params=pltpu.CompilerParams(vmem_limit_bytes=2 * 1024 * 1024),
        name="leave",
    )(hyena, attn)
    return hyena, attn.reshape(rows, heads, size)


def solution(mesh):
    in_specs = (
        P(("dp", "ctx"), None, "mp"),
        P(None, None, "mp"),
        P(None, "mp"),
        P(None, "mp"),
        P("mp"),
        P(("dp", "ctx"), "mp", None),
        P(("dp", "ctx"), "mp", None),
        P(("dp", "ctx"), "mp", None),
    )
    out_specs = (P(("dp", "ctx"), "mp"), P(("dp", "ctx"), "mp", None))
    return jax.shard_map(functools.partial(body, mesh.shape["ctx"]), mesh=mesh,
                         in_specs=in_specs, out_specs=out_specs, check_vma=False)
```

```python
import functools
import math

import jax
import jax.numpy as jnp
from jax import lax
from jax.experimental import pallas as pl
from jax.experimental.pallas import tpu as pltpu
from jax.sharding import PartitionSpec as P

GSIZE = 16
LANES = 128
EDGE = 8
HEAD_ROWS = 16
MESH = pl.DeviceIdType.MESH
BF16 = jnp.bfloat16
F32 = jnp.float32


def iota(shape, axis):
    return lax.broadcasted_iota(jnp.int32, shape, axis)


def dot(a, b):
    return jnp.dot(a, b, preferred_element_type=F32)


def dot_nt(a, b):
    return lax.dot_general(a, b, (((1,), (1,)), ((), ())), preferred_element_type=F32)


def split_f32(value):
    high = value.astype(BF16).astype(F32)
    return high, value - high


def kernel(
    n, heads, chunk,
    streams, taps_in, residue_in, rate_in, skip_in, q_in, k_in, v_in,
    hy_v, at_v,
    taps, residue, rate, skip,
    xs, qv, kv, rim_tx, rim_rx, ext, gated, mixed, rates, residues, skips, tapx, falls, decay, coeff, longt, gate,
    st_tx, st_rx, acc, big,
    in_sem, kv_send, kv_recv, rim_send, rim_recv, st_send, st_recv,
):
    me = lax.axis_index("ctx")
    rows, chans = xs.shape[1], xs.shape[2]
    modes, groups = rate.shape
    reach = taps.shape[1] - 1
    tiles = chans // LANES
    per = LANES // GSIZE
    half = chans // 2

    in_copies = [
        pltpu.make_async_copy(streams, xs, in_sem.at[0]),
        pltpu.make_async_copy(k_in, kv.at[me, 0], in_sem.at[1]),
        pltpu.make_async_copy(v_in, kv.at[me, 1], in_sem.at[2]),
        pltpu.make_async_copy(q_in, qv, in_sem.at[3]),
        pltpu.make_async_copy(rate_in, rate, in_sem.at[4]),
        pltpu.make_async_copy(residue_in, residue, in_sem.at[5]),
        pltpu.make_async_copy(taps_in, taps, in_sem.at[6]),
        pltpu.make_async_copy(skip_in, skip, in_sem.at[7]),
    ]
    for copy in in_copies:
        copy.start()

    barrier = pltpu.get_barrier_semaphore()
    for d in range(1, n):
        @pl.when(me >= d)
        def _():
            pl.semaphore_signal(barrier, inc=1, device_id={"ctx": me - d}, device_id_type=MESH)

    def kv_copy(part, d):
        return pltpu.make_async_remote_copy(
            src_ref=k_in if part == 0 else v_in, dst_ref=kv.at[me, part],
            send_sem=kv_send.at[d, part], recv_sem=kv_recv.at[me, part],
            device_id={"ctx": me + d}, device_id_type=MESH)

    def kv_each(distances, act):
        for d in distances:
            @pl.when(me + d < n)
            def _():
                act(kv_copy(0, d))
                act(kv_copy(1, d))

    def kv_arrival(part, source):
        return pltpu.make_async_remote_copy(
            src_ref=kv.at[source, part], dst_ref=kv.at[source, part], send_sem=kv_send.at[0, part],
            recv_sem=kv_recv.at[source, part], device_id={"ctx": source}, device_id_type=MESH)

    def st_copy(d):
        return pltpu.make_async_remote_copy(
            src_ref=st_tx, dst_ref=st_rx.at[me], send_sem=st_send.at[d],
            recv_sem=st_recv.at[me], device_id={"ctx": me + d}, device_id_type=MESH)

    def st_arrival(source):
        return pltpu.make_async_remote_copy(
            src_ref=st_tx, dst_ref=st_rx.at[source], send_sem=st_send.at[0],
            recv_sem=st_recv.at[source], device_id={"ctx": source}, device_id_type=MESH)

    def rim_copy():
        return pltpu.make_async_remote_copy(
            src_ref=rim_tx, dst_ref=rim_rx, send_sem=rim_send, recv_sem=rim_recv,
            device_id={"ctx": lax.rem(me + 1, n)}, device_id_type=MESH)

    @pl.when(me < n - 1)
    def _():
        pl.semaphore_wait(barrier, n - 1 - me)

    kv_each(range(n - 1, 1, -1), lambda copy: copy.start())

    in_copies[0].wait()
    tail = xs[:, rows - HEAD_ROWS:, :].astype(F32)[:, HEAD_ROWS - EDGE:, :]
    rim_tx[:, :chans] = jnp.concatenate([tail[1], tail[2]], axis=0).astype(BF16)
    rim_tx[:, chans:] = jnp.concatenate([tail[0, :, :half], tail[0, :, half:]], axis=0).astype(BF16)

    @pl.when(me < n - 1)
    def _():
        rim_copy().start()

    kv_each((1,), lambda copy: copy.start())

    for copy in in_copies[4:]:
        copy.wait()
    spread = (iota((groups, chans), 1) // GSIZE == iota((groups, chans), 0)).astype(F32)
    spread = spread.astype(BF16)
    mixed[...] = jnp.zeros(mixed.shape, F32)
    for j in range(3):
        mixed[EDGE * j:EDGE * j + reach + 1, :] = taps[j]
    mixed[3 * EDGE:3 * EDGE + modes, :] = rate[...]
    mixed[3 * EDGE + modes:, :] = residue[...]
    whole = mixed[...]
    high, rest = split_f32(whole)
    middle, rest = split_f32(rest)
    count = 3 * EDGE + 2 * modes
    spread_out = dot(jnp.concatenate([high, middle, rest], axis=0).astype(BF16), spread)
    spread_out = (spread_out[2 * count:] + spread_out[count:2 * count]) + spread_out[:count]
    for j in range(3):
        tapx[j] = spread_out[EDGE * j:EDGE * (j + 1)]
    rate_nc = spread_out[3 * EDGE:3 * EDGE + modes]
    rates[...] = rate_nc
    residues[...] = spread_out[3 * EDGE + modes:]
    step_decay = jnp.exp(rate_nc * (-float(rows)))

    for q in range(tiles):
        skips[:1, q * LANES:(q + 1) * LANES] = skip[q * LANES:(q + 1) * LANES].reshape(1, LANES)

    def lanes_of(q):
        if isinstance(q, int):
            return pl.ds(q * LANES, LANES)
        return pl.ds(pl.multiple_of(q * LANES, LANES), LANES)

    def filtered(j, q, low, high):
        total = None
        for k in range(reach + 1):
            term = (tapx[j, k:k + 1, lanes_of(q)]
                    * ext[j * tiles + q, pl.ds(EDGE - k + low, high - low), :])
            total = term if total is None else total + term
        return total

    def fill_gated(q, low, high):
        gated[low:high, lanes_of(q)] = (
            filtered(1, q, low, high) * filtered(2, q, low, high)).astype(BF16)

    lane = iota((modes, LANES), 1).astype(F32)

    def prepare(q, carry):
        for j in range(3):
            ext[j * tiles + q, EDGE:, :] = xs[j, :, lanes_of(q)].astype(F32)
        fill_gated(q, HEAD_ROWS, rows)
        rate_v = rates[:, lanes_of(q)]
        for gg in range(per):
            rate_b = jnp.broadcast_to(rate_v[:, gg * GSIZE:gg * GSIZE + 1], (modes, LANES))
            fall = jnp.exp(rate_b * (lane - (rows - 1.0)))
            falls[q, gg * modes:(gg + 1) * modes, :] = fall
            decay[q, gg * modes:(gg + 1) * modes, :] = fall.astype(BF16)
        return carry

    lax.fori_loop(0, tiles, prepare, 0)

    @pl.when(me > 0)
    def _():
        rim_copy().wait_recv()
        edge = rim_rx[...].astype(F32)
        for q in range(tiles):
            cut = slice(q * LANES, (q + 1) * LANES)
            ext[tiles + q, :EDGE, :] = edge[:EDGE, cut]
            ext[2 * tiles + q, :EDGE, :] = edge[EDGE:, cut]
            place, row = (q, 0) if q < tiles // 2 else (q - tiles // 2, EDGE)
            ext[q, :EDGE, :] = edge[row:row + EDGE, chans + place * LANES:chans + (place + 1) * LANES]

    @pl.when(me == 0)
    def _():
        ext[:, :EDGE, :] = jnp.zeros((3 * tiles, EDGE, LANES), F32)

    for q in range(tiles):
        fill_gated(q, 0, HEAD_ROWS)

    pick = iota((modes, LANES), 1) // GSIZE
    for q in range(tiles):
        cut = slice(q * LANES, (q + 1) * LANES)
        full = dot(decay[q], gated[:, cut])
        state = jnp.zeros((modes, LANES), F32)
        for gg in range(per):
            state = jnp.where(pick == gg, full[gg * modes:(gg + 1) * modes], state)
        st_tx[:, cut] = state.astype(BF16)

    for d in range(1, n):
        @pl.when(me + d < n)
        def _():
            st_copy(d).start()

    half_rows = rows // 2
    causal = iota((half_rows, LANES), 1) <= iota((half_rows, LANES), 0) + half_rows
    picks = [(iota((1, 2 * LANES), 1) % LANES // GSIZE == gg).astype(F32).astype(BF16)
             for gg in range(per)]
    blank = jnp.zeros((half_rows, LANES), BF16)

    def near_tile(q, carry):
        rate_v = rates[:, lanes_of(q)]
        residue_v = residues[:, lanes_of(q)]
        turned, blocks = [], []
        for gg in range(per):
            one = slice(gg * GSIZE, gg * GSIZE + 1)
            rate_b = jnp.broadcast_to(rate_v[:, one], (modes, LANES))
            residue_b = jnp.broadcast_to(residue_v[:, one], (modes, LANES))
            turned.append(residue_b * jnp.exp(rate_b * (-1.0 - lane)))
            fall = falls[q, gg * modes:(gg + 1) * modes, :]
            table = jnp.sum(residue_b * fall, axis=0, keepdims=True)
            rolled = pltpu.roll(
                jnp.broadcast_to(table, (half_rows, LANES)), half_rows + 1, 1,
                stride=1, stride_axis=0)
            blocks.append(jnp.where(causal, rolled, 0.0).astype(BF16))
        own = gated[:, lanes_of(q)]
        moved = jnp.concatenate([blank, own[:half_rows]], axis=0)
        pair = jnp.concatenate([moved, own], axis=1)
        parts = jnp.concatenate([pair * picks[gg] for gg in range(per)], axis=0)
        near = dot(jnp.concatenate(blocks, axis=1), parts)
        near = jnp.concatenate([near[:, :LANES], near[:, LANES:]], axis=0)
        coeff[q] = jnp.transpose(jnp.concatenate(turned, axis=0)).astype(BF16)
        gate[:, lanes_of(q)] = filtered(0, q, 0, rows)
        longt[:, lanes_of(q)] = near + skips[:1, lanes_of(q)] * own.astype(F32)
        return carry

    lax.fori_loop(0, tiles, near_tile, 0)

    scale = math.log2(math.e) / math.sqrt(LANES)
    for copy in in_copies[1:4]:
        copy.wait()
    ones = jnp.ones((HEAD_ROWS, rows), BF16)
    wide = heads * rows
    last = LANES + EDGE

    def values_of(source):
        turned = jnp.transpose(kv[source, 1].astype(F32)).astype(BF16)
        return jnp.concatenate([turned, ones], axis=0)

    own_value = values_of(me)
    for c in range(wide // chunk):
        cut = slice(c * chunk, (c + 1) * chunk)
        seen = (c + 1) * chunk // heads
        scores = dot_nt(kv[me, 0, :seen, :], qv[cut, :])
        target = (iota((seen, chunk), 1) + c * chunk) // heads
        scores = jnp.where(iota((seen, chunk), 0) <= target, scores, -1e30)
        largest = jnp.max(scores, axis=0, keepdims=True)
        weights = jnp.exp2((scores - largest) * scale).astype(BF16)
        big[:, cut] = jnp.broadcast_to(largest, (EDGE, chunk))
        acc[:, cut] = dot(own_value[:, :seen], weights)[:last]

    def far_block(d, carry):
        source = me - d

        kv_arrival(0, source).wait_recv()
        kv_arrival(1, source).wait_recv()
        value = values_of(source)
        for c in range(wide // chunk):
            cut = slice(c * chunk, (c + 1) * chunk)
            scores = dot_nt(kv[source, 0], qv[cut, :])
            before = big[:1, cut]
            largest = jnp.maximum(before, jnp.max(scores, axis=0, keepdims=True))
            weights = jnp.exp2((scores - largest) * scale).astype(BF16)
            fix = jnp.exp2((before - largest) * scale)
            big[:, cut] = jnp.broadcast_to(largest, (EDGE, chunk))
            acc[:, cut] = acc[:, cut] * fix + dot(value, weights)[:last]
        return carry

    lax.fori_loop(1, me + 1, far_block, 0)

    def gather_state(source, state):
        st_arrival(source).wait_recv()
        return state * step_decay + st_rx[source].astype(F32)

    state = lax.fori_loop(0, me, gather_state, jnp.zeros((modes, chans), F32))
    for q in range(tiles):
        cut = slice(q * LANES, (q + 1) * LANES)
        block = jnp.concatenate(
            [jnp.where(pick == gg, state[:, cut], 0.0) for gg in range(per)], axis=0)
        far = dot(coeff[q], block.astype(BF16))
        hy_v[:, cut] = (gate[:, cut] * (longt[:, cut] + far)).astype(BF16)


    for c in range(wide // LANES):
        cut = slice(c * LANES, (c + 1) * LANES)
        ratio = acc[:LANES, cut] * (1.0 / acc[LANES:LANES + 1, cut])
        at_v[cut, :] = jnp.transpose(ratio).astype(BF16)

    @pl.when(me < n - 1)
    def _():
        rim_copy().wait_send()

    for d in range(1, n):
        @pl.when(me + d < n)
        def _():
            st_copy(d).wait_send()

    kv_each(range(1, n), lambda copy: copy.wait_send())


def leave(hy_v, at_v, hy_out, at_out, sem):
    copies = [pltpu.make_async_copy(hy_v, hy_out, sem.at[0]),
              pltpu.make_async_copy(at_v, at_out, sem.at[1])]
    for copy in copies:
        copy.start()
    for copy in copies:
        copy.wait()


def body(n, streams, short_taps, modal_residue, modal_rate, skip_gain, queries, keys, values):
    rows, _, chans = streams.shape
    heads, size = queries.shape[1], queries.shape[2]
    modes, groups = modal_rate.shape
    tiles = chans // LANES
    per = LANES // GSIZE
    wide = heads * rows
    chunk = min(256, wide)
    reach = short_taps.shape[0]
    vmem, hbm = pl.BlockSpec(memory_space=pltpu.VMEM), pl.BlockSpec(memory_space=pltpu.HBM)
    dma = pltpu.SemaphoreType.DMA
    hyena, attn = pl.pallas_call(
        functools.partial(kernel, n, heads, chunk),
        out_shape=(jax.ShapeDtypeStruct((rows, chans), BF16),
                   jax.ShapeDtypeStruct((wide, size), BF16)),
        in_specs=[hbm] * 8,
        out_specs=(vmem, vmem),
        scratch_shapes=[
            pltpu.VMEM((3, reach, groups), F32),
            pltpu.VMEM((modes, groups), F32),
            pltpu.VMEM((modes, groups), F32),
            pltpu.VMEM((chans,), F32),
            pltpu.VMEM((3, rows, chans), BF16),
            pltpu.VMEM((wide, size), BF16),
            pltpu.VMEM((n, 2, rows, size), BF16),
            pltpu.VMEM((2 * EDGE, chans + chans // 2), BF16),
            pltpu.VMEM((2 * EDGE, chans + chans // 2), BF16),
            pltpu.VMEM((3 * tiles, rows + EDGE, LANES), F32),
            pltpu.VMEM((rows, chans), BF16),
            pltpu.VMEM((3 * EDGE + 2 * modes, groups), F32),
            pltpu.VMEM((modes, chans), F32),
            pltpu.VMEM((modes, chans), F32),
            pltpu.VMEM((EDGE, chans), F32),
            pltpu.VMEM((3, EDGE, chans), F32),
            pltpu.VMEM((tiles, LANES, LANES), F32),
            pltpu.VMEM((tiles, LANES, LANES), BF16),
            pltpu.VMEM((tiles, LANES, LANES), BF16),
            pltpu.VMEM((rows, chans), F32),
            pltpu.VMEM((rows, chans), F32),
            pltpu.VMEM((modes, chans), BF16),
            pltpu.VMEM((n, modes, chans), BF16),
            pltpu.VMEM((size + EDGE, wide), F32),
            pltpu.VMEM((EDGE, wide), F32),
            dma((8,)), dma((n, 2)), dma((n, 2)),
            dma, dma, dma((n,)), dma((n,)),
        ],
        compiler_params=pltpu.CompilerParams(
            collective_id=0, has_side_effects=True, vmem_limit_bytes=40 * 1024 * 1024),
        name="mixers",
    )(*[pltpu.with_memory_space_constraint(x, pltpu.HBM) for x in (
        jnp.transpose(streams, (1, 0, 2)),
        jnp.transpose(short_taps, (1, 0, 2)),
        modal_residue,
        modal_rate,
        skip_gain,
        queries.reshape(wide, size),
        keys.reshape(rows, size),
        values.reshape(rows, size),
    )])
    hyena, attn = pl.pallas_call(
        leave,
        out_shape=(jax.ShapeDtypeStruct((rows, chans), BF16),
                   jax.ShapeDtypeStruct((wide, size), BF16)),
        in_specs=[vmem, vmem],
        out_specs=(hbm, hbm),
        scratch_shapes=[dma((2,))],
        compiler_params=pltpu.CompilerParams(vmem_limit_bytes=2 * 1024 * 1024),
        name="leave",
    )(hyena, attn)
    return hyena, attn.reshape(rows, heads, size)


def solution(mesh):
    in_specs = (
        P(("dp", "ctx"), None, "mp"),
        P(None, None, "mp"),
        P(None, "mp"),
        P(None, "mp"),
        P("mp"),
        P(("dp", "ctx"), "mp", None),
        P(("dp", "ctx"), "mp", None),
        P(("dp", "ctx"), "mp", None),
    )
    out_specs = (P(("dp", "ctx"), "mp"), P(("dp", "ctx"), "mp", None))
    return jax.shard_map(functools.partial(body, mesh.shape["ctx"]), mesh=mesh,
                         in_specs=in_specs, out_specs=out_specs, check_vma=False)
```

```python
import functools
import math

import jax
import jax.numpy as jnp
from jax import lax
from jax.experimental import pallas as pl
from jax.experimental.pallas import tpu as pltpu
from jax.sharding import PartitionSpec as P

GSIZE = 16
LANES = 128
EDGE = 8
HEAD_ROWS = 16
MESH = pl.DeviceIdType.MESH
BF16 = jnp.bfloat16
F32 = jnp.float32


def iota(shape, axis):
    return lax.broadcasted_iota(jnp.int32, shape, axis)


def dot(a, b):
    return jnp.dot(a, b, preferred_element_type=F32)


def dot_nt(a, b):
    return lax.dot_general(a, b, (((1,), (1,)), ((), ())), preferred_element_type=F32)


def split_f32(value):
    high = value.astype(BF16).astype(F32)
    return high, value - high


def kernel(
    n, heads, chunk,
    streams, taps_in, residue_in, rate_in, skip_in, q_in, k_in, v_in,
    hy_v, at_v,
    taps, residue, rate, skip,
    xs, qv, kv, rim_tx, rim_rx, ext, gated, mixed, rates, residues, skips, tapx, falls, decay, coeff, longt, gate,
    st_tx, st_rx, run_p, run_e, acc, big,
    in_sem, kv_send, kv_recv, rim_send, rim_recv, st_send, st_recv,
):
    me = lax.axis_index("ctx")
    rows, chans = xs.shape[1], xs.shape[2]
    modes, groups = rate.shape
    reach = taps.shape[1] - 1
    tiles = chans // LANES
    per = LANES // GSIZE
    half = chans // 2

    in_copies = [
        pltpu.make_async_copy(streams, xs, in_sem.at[0]),
        pltpu.make_async_copy(k_in, kv.at[me, 0], in_sem.at[1]),
        pltpu.make_async_copy(v_in, kv.at[me, 1], in_sem.at[2]),
        pltpu.make_async_copy(q_in, qv, in_sem.at[3]),
        pltpu.make_async_copy(rate_in, rate, in_sem.at[4]),
        pltpu.make_async_copy(residue_in, residue, in_sem.at[5]),
        pltpu.make_async_copy(taps_in, taps, in_sem.at[6]),
        pltpu.make_async_copy(skip_in, skip, in_sem.at[7]),
    ]
    for copy in in_copies:
        copy.start()

    barrier = pltpu.get_barrier_semaphore()
    for d in range(1, n):
        @pl.when(me >= d)
        def _():
            pl.semaphore_signal(barrier, inc=1, device_id={"ctx": me - d}, device_id_type=MESH)

    def kv_copy(part, source, own):
        src = (k_in if part == 0 else v_in) if own else kv.at[source, part]
        return pltpu.make_async_remote_copy(
            src_ref=src, dst_ref=kv.at[source, part], send_sem=kv_send.at[source, part],
            recv_sem=kv_recv.at[source, part], device_id={"ctx": lax.rem(me + 1, n)},
            device_id_type=MESH)

    def kv_arrival(part, source):
        return pltpu.make_async_remote_copy(
            src_ref=kv.at[source, part], dst_ref=kv.at[source, part], send_sem=kv_send.at[source, part],
            recv_sem=kv_recv.at[source, part], device_id={"ctx": source}, device_id_type=MESH)

    steps = (n - 1).bit_length()

    def st_copy(k):
        return pltpu.make_async_remote_copy(
            src_ref=st_tx.at[k], dst_ref=st_rx.at[k], send_sem=st_send.at[k],
            recv_sem=st_recv.at[k], device_id={"ctx": lax.rem(me + 2 ** k, n)},
            device_id_type=MESH)

    def st_out(k):
        st_tx[k] = run_p[...].astype(BF16)

        @pl.when(me + 2 ** k < n)
        def _():
            st_copy(k).start()

    def st_in(k):
        @pl.when(me >= 2 ** k)
        def _():
            st_copy(k).wait_recv()
            got = st_rx[k].astype(F32)
            fall = -float(rows) * rates[...]
            run_e[...] += got if k == 0 else got * jnp.exp(fall * (2 ** k - 1.0))
            if k + 1 < steps:
                run_p[...] += got * jnp.exp(fall * float(2 ** k))

    def rim_copy():
        return pltpu.make_async_remote_copy(
            src_ref=rim_tx, dst_ref=rim_rx, send_sem=rim_send, recv_sem=rim_recv,
            device_id={"ctx": lax.rem(me + 1, n)}, device_id_type=MESH)

    in_copies[0].wait()
    tail = xs[:, rows - HEAD_ROWS:, :].astype(F32)[:, HEAD_ROWS - EDGE:, :]
    rim_tx[:, :chans] = jnp.concatenate([tail[1], tail[2]], axis=0).astype(BF16)
    rim_tx[:, chans:] = jnp.concatenate([tail[0, :, :half], tail[0, :, half:]], axis=0).astype(BF16)

    @pl.when(me < n - 1)
    def _():
        pl.semaphore_wait(barrier, n - 1 - me)
        rim_copy().start()

    @pl.when(me < n - 1)
    def _():
        kv_copy(0, me, True).start()
        kv_copy(1, me, True).start()

    for copy in in_copies[4:]:
        copy.wait()
    spread = (iota((groups, chans), 1) // GSIZE == iota((groups, chans), 0)).astype(F32)
    spread = spread.astype(BF16)
    mixed[...] = jnp.zeros(mixed.shape, F32)
    for j in range(3):
        mixed[EDGE * j:EDGE * j + reach + 1, :] = taps[j]
    mixed[3 * EDGE:3 * EDGE + modes, :] = rate[...]
    mixed[3 * EDGE + modes:, :] = residue[...]
    whole = mixed[...]
    high, rest = split_f32(whole)
    middle, rest = split_f32(rest)
    count = 3 * EDGE + 2 * modes
    spread_out = dot(jnp.concatenate([high, middle, rest], axis=0).astype(BF16), spread)
    spread_out = (spread_out[2 * count:] + spread_out[count:2 * count]) + spread_out[:count]
    for j in range(3):
        tapx[j] = spread_out[EDGE * j:EDGE * (j + 1)]
    rate_nc = spread_out[3 * EDGE:3 * EDGE + modes]
    rates[...] = rate_nc
    residues[...] = spread_out[3 * EDGE + modes:]

    for q in range(tiles):
        skips[:1, q * LANES:(q + 1) * LANES] = skip[q * LANES:(q + 1) * LANES].reshape(1, LANES)

    def lanes_of(q):
        if isinstance(q, int):
            return pl.ds(q * LANES, LANES)
        return pl.ds(pl.multiple_of(q * LANES, LANES), LANES)

    def filtered(j, q, low, high):
        total = None
        for k in range(reach + 1):
            term = (tapx[j, k:k + 1, lanes_of(q)]
                    * ext[j * tiles + q, pl.ds(EDGE - k + low, high - low), :])
            total = term if total is None else total + term
        return total

    def fill_gated(q, low, high):
        gated[low:high, lanes_of(q)] = (
            filtered(1, q, low, high) * filtered(2, q, low, high)).astype(BF16)

    lane = iota((modes, LANES), 1).astype(F32)

    def prepare(q, carry):
        for j in range(3):
            ext[j * tiles + q, EDGE:, :] = xs[j, :, lanes_of(q)].astype(F32)
        fill_gated(q, HEAD_ROWS, rows)
        rate_v = rates[:, lanes_of(q)]
        for gg in range(per):
            rate_b = jnp.broadcast_to(rate_v[:, gg * GSIZE:gg * GSIZE + 1], (modes, LANES))
            fall = jnp.exp(rate_b * (lane - (rows - 1.0)))
            falls[q, gg * modes:(gg + 1) * modes, :] = fall
            decay[q, gg * modes:(gg + 1) * modes, :] = fall.astype(BF16)
        return carry

    lax.fori_loop(0, tiles, prepare, 0)

    @pl.when(me > 0)
    def _():
        rim_copy().wait_recv()
        edge = rim_rx[...].astype(F32)
        for q in range(tiles):
            cut = slice(q * LANES, (q + 1) * LANES)
            ext[tiles + q, :EDGE, :] = edge[:EDGE, cut]
            ext[2 * tiles + q, :EDGE, :] = edge[EDGE:, cut]
            place, row = (q, 0) if q < tiles // 2 else (q - tiles // 2, EDGE)
            ext[q, :EDGE, :] = edge[row:row + EDGE, chans + place * LANES:chans + (place + 1) * LANES]

    @pl.when(me == 0)
    def _():
        ext[:, :EDGE, :] = jnp.zeros((3 * tiles, EDGE, LANES), F32)

    for q in range(tiles):
        fill_gated(q, 0, HEAD_ROWS)

    pick = iota((modes, LANES), 1) // GSIZE
    for q in range(tiles):
        cut = slice(q * LANES, (q + 1) * LANES)
        full = dot(decay[q], gated[:, cut])
        state = jnp.zeros((modes, LANES), F32)
        for gg in range(per):
            state = jnp.where(pick == gg, full[gg * modes:(gg + 1) * modes], state)
        run_p[:, cut] = state
    run_e[...] = jnp.zeros(run_e.shape, F32)
    st_out(0)

    half_rows = rows // 2
    causal = iota((half_rows, LANES), 1) <= iota((half_rows, LANES), 0) + half_rows
    picks = [(iota((1, 2 * LANES), 1) % LANES // GSIZE == gg).astype(F32).astype(BF16)
             for gg in range(per)]
    blank = jnp.zeros((half_rows, LANES), BF16)

    def pass_on(source):
        for part in range(2):
            kv_arrival(part, source).wait_recv()
            kv_copy(part, source, False).start()

    def near_tile(q, carry):
        @pl.when((q == tiles - 2) & (me > 0) & (me < n - 1))
        def _():
            pass_on(me - 1)

        rate_v = rates[:, lanes_of(q)]
        residue_v = residues[:, lanes_of(q)]
        turned, blocks = [], []
        for gg in range(per):
            one = slice(gg * GSIZE, gg * GSIZE + 1)
            rate_b = jnp.broadcast_to(rate_v[:, one], (modes, LANES))
            residue_b = jnp.broadcast_to(residue_v[:, one], (modes, LANES))
            turned.append(residue_b * jnp.exp(rate_b * (-1.0 - lane)))
            fall = falls[q, gg * modes:(gg + 1) * modes, :]
            table = jnp.sum(residue_b * fall, axis=0, keepdims=True)
            rolled = pltpu.roll(
                jnp.broadcast_to(table, (half_rows, LANES)), half_rows + 1, 1,
                stride=1, stride_axis=0)
            blocks.append(jnp.where(causal, rolled, 0.0).astype(BF16))
        own = gated[:, lanes_of(q)]
        moved = jnp.concatenate([blank, own[:half_rows]], axis=0)
        pair = jnp.concatenate([moved, own], axis=1)
        parts = jnp.concatenate([pair * picks[gg] for gg in range(per)], axis=0)
        near = dot(jnp.concatenate(blocks, axis=1), parts)
        near = jnp.concatenate([near[:, :LANES], near[:, LANES:]], axis=0)
        coeff[q] = jnp.transpose(jnp.concatenate(turned, axis=0)).astype(BF16)
        gate[:, lanes_of(q)] = filtered(0, q, 0, rows)
        longt[:, lanes_of(q)] = near + skips[:1, lanes_of(q)] * own.astype(F32)
        return carry

    lax.fori_loop(0, tiles, near_tile, 0)

    for k in range(steps - 1):
        @pl.when(me + 2 ** (k + 1) < n)
        def _():
            st_in(k)
            st_out(k + 1)

    scale = math.log2(math.e) / math.sqrt(LANES)
    for copy in in_copies[1:4]:
        copy.wait()
    ones = jnp.ones((HEAD_ROWS, rows), BF16)
    wide = heads * rows
    last = LANES + EDGE

    def values_of(source):
        turned = jnp.transpose(kv[source, 1].astype(F32)).astype(BF16)
        return jnp.concatenate([turned, ones], axis=0)

    own_value = values_of(me)
    for c in range(wide // chunk):
        cut = slice(c * chunk, (c + 1) * chunk)
        seen = (c + 1) * chunk // heads
        scores = dot_nt(kv[me, 0, :seen, :], qv[cut, :])
        target = (iota((seen, chunk), 1) + c * chunk) // heads
        scores = jnp.where(iota((seen, chunk), 0) <= target, scores, -1e30)
        largest = jnp.max(scores, axis=0, keepdims=True)
        weights = jnp.exp2((scores - largest) * scale).astype(BF16)
        big[:, cut] = jnp.broadcast_to(largest, (EDGE, chunk))
        acc[:, cut] = dot(own_value[:, :seen], weights)[:last]

    def far_block(d, carry):
        source = me - d

        @pl.when((me < n - 1) & (d < me))
        def _():
            pass_on(source - 1)

        @pl.when(me == n - 1)
        def _():
            kv_arrival(0, source).wait_recv()
            kv_arrival(1, source).wait_recv()

        value = values_of(source)
        for c in range(wide // chunk):
            cut = slice(c * chunk, (c + 1) * chunk)
            scores = dot_nt(kv[source, 0], qv[cut, :])
            before = big[:1, cut]
            largest = jnp.maximum(before, jnp.max(scores, axis=0, keepdims=True))
            weights = jnp.exp2((scores - largest) * scale).astype(BF16)
            fix = jnp.exp2((before - largest) * scale)
            big[:, cut] = jnp.broadcast_to(largest, (EDGE, chunk))
            acc[:, cut] = acc[:, cut] * fix + dot(value, weights)[:last]
        return carry

    middle = jnp.maximum(me, jnp.minimum(me + 1, 2))
    lax.fori_loop(1, middle, far_block, 0)

    for k in range(steps):
        @pl.when(me + 2 ** (k + 1) >= n)
        def _():
            st_in(k)

    for q in range(tiles):
        cut = slice(q * LANES, (q + 1) * LANES)
        block = jnp.concatenate(
            [jnp.where(pick == gg, run_e[:, cut], 0.0) for gg in range(per)], axis=0)
        far = dot(coeff[q], block.astype(BF16))
        hy_v[:, cut] = (gate[:, cut] * (longt[:, cut] + far)).astype(BF16)

    lax.fori_loop(middle, me + 1, far_block, 0)

    for c in range(wide // LANES):
        cut = slice(c * LANES, (c + 1) * LANES)
        ratio = acc[:LANES, cut] * (1.0 / acc[LANES:LANES + 1, cut])
        at_v[cut, :] = jnp.transpose(ratio).astype(BF16)

    @pl.when(me < n - 1)
    def _():
        rim_copy().wait_send()

    for k in range(steps):
        @pl.when(me + 2 ** k < n)
        def _():
            st_copy(k).wait_send()

    def sent(source, carry):
        kv_copy(0, source, False).wait_send()
        kv_copy(1, source, False).wait_send()
        return carry

    @pl.when(me < n - 1)
    def _():
        kv_copy(0, me, True).wait_send()
        kv_copy(1, me, True).wait_send()
        lax.fori_loop(0, me, sent, 0)


def leave(hy_v, at_v, hy_out, at_out, sem):
    copies = [pltpu.make_async_copy(hy_v, hy_out, sem.at[0]),
              pltpu.make_async_copy(at_v, at_out, sem.at[1])]
    for copy in copies:
        copy.start()
    for copy in copies:
        copy.wait()


def body(n, streams, short_taps, modal_residue, modal_rate, skip_gain, queries, keys, values):
    rows, _, chans = streams.shape
    heads, size = queries.shape[1], queries.shape[2]
    modes, groups = modal_rate.shape
    tiles = chans // LANES
    per = LANES // GSIZE
    wide = heads * rows
    chunk = min(256, wide)
    reach = short_taps.shape[0]
    steps = (n - 1).bit_length()
    vmem, hbm = pl.BlockSpec(memory_space=pltpu.VMEM), pl.BlockSpec(memory_space=pltpu.HBM)
    dma = pltpu.SemaphoreType.DMA
    hyena, attn = pl.pallas_call(
        functools.partial(kernel, n, heads, chunk),
        out_shape=(jax.ShapeDtypeStruct((rows, chans), BF16),
                   jax.ShapeDtypeStruct((wide, size), BF16)),
        in_specs=[hbm] * 8,
        out_specs=(vmem, vmem),
        scratch_shapes=[
            pltpu.VMEM((3, reach, groups), F32),
            pltpu.VMEM((modes, groups), F32),
            pltpu.VMEM((modes, groups), F32),
            pltpu.VMEM((chans,), F32),
            pltpu.VMEM((3, rows, chans), BF16),
            pltpu.VMEM((wide, size), BF16),
            pltpu.VMEM((n, 2, rows, size), BF16),
            pltpu.VMEM((2 * EDGE, chans + chans // 2), BF16),
            pltpu.VMEM((2 * EDGE, chans + chans // 2), BF16),
            pltpu.VMEM((3 * tiles, rows + EDGE, LANES), F32),
            pltpu.VMEM((rows, chans), BF16),
            pltpu.VMEM((3 * EDGE + 2 * modes, groups), F32),
            pltpu.VMEM((modes, chans), F32),
            pltpu.VMEM((modes, chans), F32),
            pltpu.VMEM((EDGE, chans), F32),
            pltpu.VMEM((3, EDGE, chans), F32),
            pltpu.VMEM((tiles, LANES, LANES), F32),
            pltpu.VMEM((tiles, LANES, LANES), BF16),
            pltpu.VMEM((tiles, LANES, LANES), BF16),
            pltpu.VMEM((rows, chans), F32),
            pltpu.VMEM((rows, chans), F32),
            pltpu.VMEM((steps, modes, chans), BF16),
            pltpu.VMEM((steps, modes, chans), BF16),
            pltpu.VMEM((modes, chans), F32),
            pltpu.VMEM((modes, chans), F32),
            pltpu.VMEM((size + EDGE, wide), F32),
            pltpu.VMEM((EDGE, wide), F32),
            dma((8,)), dma((n, 2)), dma((n, 2)),
            dma, dma, dma((steps,)), dma((steps,)),
        ],
        compiler_params=pltpu.CompilerParams(
            collective_id=0, has_side_effects=True, vmem_limit_bytes=40 * 1024 * 1024),
        name="mixers",
    )(*[pltpu.with_memory_space_constraint(x, pltpu.HBM) for x in (
        jnp.transpose(streams, (1, 0, 2)),
        jnp.transpose(short_taps, (1, 0, 2)),
        modal_residue,
        modal_rate,
        skip_gain,
        queries.reshape(wide, size),
        keys.reshape(rows, size),
        values.reshape(rows, size),
    )])
    hyena, attn = pl.pallas_call(
        leave,
        out_shape=(jax.ShapeDtypeStruct((rows, chans), BF16),
                   jax.ShapeDtypeStruct((wide, size), BF16)),
        in_specs=[vmem, vmem],
        out_specs=(hbm, hbm),
        scratch_shapes=[dma((2,))],
        compiler_params=pltpu.CompilerParams(vmem_limit_bytes=2 * 1024 * 1024),
        name="leave",
    )(hyena, attn)
    return hyena, attn.reshape(rows, heads, size)


def solution(mesh):
    in_specs = (
        P(("dp", "ctx"), None, "mp"),
        P(None, None, "mp"),
        P(None, "mp"),
        P(None, "mp"),
        P("mp"),
        P(("dp", "ctx"), "mp", None),
        P(("dp", "ctx"), "mp", None),
        P(("dp", "ctx"), "mp", None),
    )
    out_specs = (P(("dp", "ctx"), "mp"), P(("dp", "ctx"), "mp", None))
    return jax.shard_map(functools.partial(body, mesh.shape["ctx"]), mesh=mesh,
                         in_specs=in_specs, out_specs=out_specs, check_vma=False)
```

```python
import functools
import math

import jax
import jax.numpy as jnp
from jax import lax
from jax.experimental import pallas as pl
from jax.experimental.pallas import tpu as pltpu
from jax.sharding import PartitionSpec as P

GSIZE = 16
LANES = 128
EDGE = 8
HEAD_ROWS = 16
MESH = pl.DeviceIdType.MESH
BF16 = jnp.bfloat16
F32 = jnp.float32


def iota(shape, axis):
    return lax.broadcasted_iota(jnp.int32, shape, axis)


def dot(a, b):
    return jnp.dot(a, b, preferred_element_type=F32)


def dot_nt(a, b):
    return lax.dot_general(a, b, (((1,), (1,)), ((), ())), preferred_element_type=F32)


def split_f32(value):
    high = value.astype(BF16).astype(F32)
    return high, value - high


def kernel(
    n, heads, chunk,
    streams, taps_in, residue_in, rate_in, skip_in, q_in, k_in, v_in,
    hy_v, at_v,
    taps, residue, rate, skip,
    xs, qv, kv, rim_tx, rim_rx, ext, gated, mixed, rates, residues, skips, tapx, falls, decay, coeff, longt, gate,
    st_tx, st_rx, acc, big,
    in_sem, kv_send, kv_recv, rim_send, rim_recv, st_send, st_recv,
):
    me = lax.axis_index("ctx")
    rows, chans = xs.shape[1], xs.shape[2]
    modes, groups = rate.shape
    reach = taps.shape[1] - 1
    tiles = chans // LANES
    per = LANES // GSIZE
    half = chans // 2

    in_copies = [
        pltpu.make_async_copy(streams, xs, in_sem.at[0]),
        pltpu.make_async_copy(k_in, kv.at[me, 0], in_sem.at[1]),
        pltpu.make_async_copy(v_in, kv.at[me, 1], in_sem.at[2]),
        pltpu.make_async_copy(q_in, qv, in_sem.at[3]),
        pltpu.make_async_copy(rate_in, rate, in_sem.at[4]),
        pltpu.make_async_copy(residue_in, residue, in_sem.at[5]),
        pltpu.make_async_copy(taps_in, taps, in_sem.at[6]),
        pltpu.make_async_copy(skip_in, skip, in_sem.at[7]),
    ]
    for copy in in_copies:
        copy.start()

    barrier = pltpu.get_barrier_semaphore()
    for d in range(1, n):
        @pl.when(me >= d)
        def _():
            pl.semaphore_signal(barrier, inc=1, device_id={"ctx": me - d}, device_id_type=MESH)

    def kv_copy(part, source, d, own=False):
        src = (k_in if part == 0 else v_in) if own else kv.at[source, part]
        return pltpu.make_async_remote_copy(
            src_ref=src, dst_ref=kv.at[source, part], send_sem=kv_send.at[source, d - 1, part],
            recv_sem=kv_recv.at[source, part], device_id={"ctx": me + d}, device_id_type=MESH)

    def kv_each(source, own, act):
        for d in (2, 1):
            @pl.when(me + d < n)
            def _():
                act(kv_copy(0, source, d, own))
                act(kv_copy(1, source, d, own))

    def kv_arrival(part, source):
        return pltpu.make_async_remote_copy(
            src_ref=kv.at[source, part], dst_ref=kv.at[source, part], send_sem=kv_send.at[source, 0, part],
            recv_sem=kv_recv.at[source, part], device_id={"ctx": source}, device_id_type=MESH)

    def st_copy(d):
        return pltpu.make_async_remote_copy(
            src_ref=st_tx, dst_ref=st_rx.at[me], send_sem=st_send.at[d],
            recv_sem=st_recv.at[me], device_id={"ctx": me + d}, device_id_type=MESH)

    def st_arrival(source):
        return pltpu.make_async_remote_copy(
            src_ref=st_tx, dst_ref=st_rx.at[source], send_sem=st_send.at[0],
            recv_sem=st_recv.at[source], device_id={"ctx": source}, device_id_type=MESH)

    def rim_copy():
        return pltpu.make_async_remote_copy(
            src_ref=rim_tx, dst_ref=rim_rx, send_sem=rim_send, recv_sem=rim_recv,
            device_id={"ctx": lax.rem(me + 1, n)}, device_id_type=MESH)

    in_copies[0].wait()
    tail = xs[:, rows - HEAD_ROWS:, :].astype(F32)[:, HEAD_ROWS - EDGE:, :]
    rim_tx[:, :chans] = jnp.concatenate([tail[1], tail[2]], axis=0).astype(BF16)
    rim_tx[:, chans:] = jnp.concatenate([tail[0, :, :half], tail[0, :, half:]], axis=0).astype(BF16)

    @pl.when(me < n - 1)
    def _():
        pl.semaphore_wait(barrier, n - 1 - me)
        rim_copy().start()

    kv_each(me, True, lambda copy: copy.start())

    for copy in in_copies[4:]:
        copy.wait()
    spread = (iota((groups, chans), 1) // GSIZE == iota((groups, chans), 0)).astype(F32)
    spread = spread.astype(BF16)
    mixed[...] = jnp.zeros(mixed.shape, F32)
    for j in range(3):
        mixed[EDGE * j:EDGE * j + reach + 1, :] = taps[j]
    mixed[3 * EDGE:3 * EDGE + modes, :] = rate[...]
    mixed[3 * EDGE + modes:, :] = residue[...]
    whole = mixed[...]
    high, rest = split_f32(whole)
    middle, rest = split_f32(rest)
    count = 3 * EDGE + 2 * modes
    spread_out = dot(jnp.concatenate([high, middle, rest], axis=0).astype(BF16), spread)
    spread_out = (spread_out[2 * count:] + spread_out[count:2 * count]) + spread_out[:count]
    for j in range(3):
        tapx[j] = spread_out[EDGE * j:EDGE * (j + 1)]
    rate_nc = spread_out[3 * EDGE:3 * EDGE + modes]
    rates[...] = rate_nc
    residues[...] = spread_out[3 * EDGE + modes:]
    step_decay = jnp.exp(rate_nc * (-float(rows)))

    for q in range(tiles):
        skips[:1, q * LANES:(q + 1) * LANES] = skip[q * LANES:(q + 1) * LANES].reshape(1, LANES)

    def lanes_of(q):
        if isinstance(q, int):
            return pl.ds(q * LANES, LANES)
        return pl.ds(pl.multiple_of(q * LANES, LANES), LANES)

    def filtered(j, q, low, high):
        total = None
        for k in range(reach + 1):
            term = (tapx[j, k:k + 1, lanes_of(q)]
                    * ext[j * tiles + q, pl.ds(EDGE - k + low, high - low), :])
            total = term if total is None else total + term
        return total

    def fill_gated(q, low, high):
        gated[low:high, lanes_of(q)] = (
            filtered(1, q, low, high) * filtered(2, q, low, high)).astype(BF16)

    lane = iota((modes, LANES), 1).astype(F32)

    def prepare(q, carry):
        for j in range(3):
            ext[j * tiles + q, EDGE:, :] = xs[j, :, lanes_of(q)].astype(F32)
        fill_gated(q, HEAD_ROWS, rows)
        rate_v = rates[:, lanes_of(q)]
        for gg in range(per):
            rate_b = jnp.broadcast_to(rate_v[:, gg * GSIZE:gg * GSIZE + 1], (modes, LANES))
            fall = jnp.exp(rate_b * (lane - (rows - 1.0)))
            falls[q, gg * modes:(gg + 1) * modes, :] = fall
            decay[q, gg * modes:(gg + 1) * modes, :] = fall.astype(BF16)
        return carry

    lax.fori_loop(0, tiles, prepare, 0)

    @pl.when(me > 0)
    def _():
        rim_copy().wait_recv()
        edge = rim_rx[...].astype(F32)
        for q in range(tiles):
            cut = slice(q * LANES, (q + 1) * LANES)
            ext[tiles + q, :EDGE, :] = edge[:EDGE, cut]
            ext[2 * tiles + q, :EDGE, :] = edge[EDGE:, cut]
            place, row = (q, 0) if q < tiles // 2 else (q - tiles // 2, EDGE)
            ext[q, :EDGE, :] = edge[row:row + EDGE, chans + place * LANES:chans + (place + 1) * LANES]

    @pl.when(me == 0)
    def _():
        ext[:, :EDGE, :] = jnp.zeros((3 * tiles, EDGE, LANES), F32)

    for q in range(tiles):
        fill_gated(q, 0, HEAD_ROWS)

    pick = iota((modes, LANES), 1) // GSIZE
    for q in range(tiles):
        cut = slice(q * LANES, (q + 1) * LANES)
        full = dot(decay[q], gated[:, cut])
        state = jnp.zeros((modes, LANES), F32)
        for gg in range(per):
            state = jnp.where(pick == gg, full[gg * modes:(gg + 1) * modes], state)
        st_tx[:, cut] = state.astype(BF16)

    for d in range(1, n):
        @pl.when(me + d < n)
        def _():
            st_copy(d).start()

    half_rows = rows // 2
    causal = iota((half_rows, LANES), 1) <= iota((half_rows, LANES), 0) + half_rows
    picks = [(iota((1, 2 * LANES), 1) % LANES // GSIZE == gg).astype(F32).astype(BF16)
             for gg in range(per)]
    blank = jnp.zeros((half_rows, LANES), BF16)

    def forward(k, carry):
        source = me - 2 * k
        kv_arrival(0, source).wait_recv()
        kv_arrival(1, source).wait_recv()
        kv_each(source, False, lambda copy: copy.start())
        return carry

    def near_tile(q, carry):
        @pl.when((q == tiles - 2) & (me < n - 1))
        def _():
            lax.fori_loop(1, me // 2 + 1, forward, 0)

        rate_v = rates[:, lanes_of(q)]
        residue_v = residues[:, lanes_of(q)]
        turned, blocks = [], []
        for gg in range(per):
            one = slice(gg * GSIZE, gg * GSIZE + 1)
            rate_b = jnp.broadcast_to(rate_v[:, one], (modes, LANES))
            residue_b = jnp.broadcast_to(residue_v[:, one], (modes, LANES))
            turned.append(residue_b * jnp.exp(rate_b * (-1.0 - lane)))
            fall = falls[q, gg * modes:(gg + 1) * modes, :]
            table = jnp.sum(residue_b * fall, axis=0, keepdims=True)
            rolled = pltpu.roll(
                jnp.broadcast_to(table, (half_rows, LANES)), half_rows + 1, 1,
                stride=1, stride_axis=0)
            blocks.append(jnp.where(causal, rolled, 0.0).astype(BF16))
        own = gated[:, lanes_of(q)]
        moved = jnp.concatenate([blank, own[:half_rows]], axis=0)
        pair = jnp.concatenate([moved, own], axis=1)
        parts = jnp.concatenate([pair * picks[gg] for gg in range(per)], axis=0)
        near = dot(jnp.concatenate(blocks, axis=1), parts)
        near = jnp.concatenate([near[:, :LANES], near[:, LANES:]], axis=0)
        coeff[q] = jnp.transpose(jnp.concatenate(turned, axis=0)).astype(BF16)
        gate[:, lanes_of(q)] = filtered(0, q, 0, rows)
        longt[:, lanes_of(q)] = near + skips[:1, lanes_of(q)] * own.astype(F32)
        return carry

    lax.fori_loop(0, tiles, near_tile, 0)

    scale = math.log2(math.e) / math.sqrt(LANES)
    for copy in in_copies[1:4]:
        copy.wait()
    ones = jnp.ones((HEAD_ROWS, rows), BF16)
    wide = heads * rows
    last = LANES + EDGE

    def values_of(source):
        turned = jnp.transpose(kv[source, 1].astype(F32)).astype(BF16)
        return jnp.concatenate([turned, ones], axis=0)

    own_value = values_of(me)
    for c in range(wide // chunk):
        cut = slice(c * chunk, (c + 1) * chunk)
        seen = (c + 1) * chunk // heads
        scores = dot_nt(kv[me, 0, :seen, :], qv[cut, :])
        target = (iota((seen, chunk), 1) + c * chunk) // heads
        scores = jnp.where(iota((seen, chunk), 0) <= target, scores, -1e30)
        largest = jnp.max(scores, axis=0, keepdims=True)
        weights = jnp.exp2((scores - largest) * scale).astype(BF16)
        big[:, cut] = jnp.broadcast_to(largest, (EDGE, chunk))
        acc[:, cut] = dot(own_value[:, :seen], weights)[:last]

    def far_block(d, carry):
        source = me - d

        @pl.when((lax.rem(d, 2) == 1) | (me == n - 1))
        def _():
            kv_arrival(0, source).wait_recv()
            kv_arrival(1, source).wait_recv()

        value = values_of(source)
        for c in range(wide // chunk):
            cut = slice(c * chunk, (c + 1) * chunk)
            scores = dot_nt(kv[source, 0], qv[cut, :])
            before = big[:1, cut]
            largest = jnp.maximum(before, jnp.max(scores, axis=0, keepdims=True))
            weights = jnp.exp2((scores - largest) * scale).astype(BF16)
            fix = jnp.exp2((before - largest) * scale)
            big[:, cut] = jnp.broadcast_to(largest, (EDGE, chunk))
            acc[:, cut] = acc[:, cut] * fix + dot(value, weights)[:last]
        return carry

    middle = jnp.maximum(me, jnp.minimum(me + 1, 2))
    lax.fori_loop(1, middle, far_block, 0)

    def gather_state(source, state):
        st_arrival(source).wait_recv()
        return state * step_decay + st_rx[source].astype(F32)

    state = lax.fori_loop(0, me, gather_state, jnp.zeros((modes, chans), F32))
    for q in range(tiles):
        cut = slice(q * LANES, (q + 1) * LANES)
        block = jnp.concatenate(
            [jnp.where(pick == gg, state[:, cut], 0.0) for gg in range(per)], axis=0)
        far = dot(coeff[q], block.astype(BF16))
        hy_v[:, cut] = (gate[:, cut] * (longt[:, cut] + far)).astype(BF16)

    lax.fori_loop(middle, me + 1, far_block, 0)

    for c in range(wide // LANES):
        cut = slice(c * LANES, (c + 1) * LANES)
        ratio = acc[:LANES, cut] * (1.0 / acc[LANES:LANES + 1, cut])
        at_v[cut, :] = jnp.transpose(ratio).astype(BF16)

    @pl.when(me < n - 1)
    def _():
        rim_copy().wait_send()

    for d in range(1, n):
        @pl.when(me + d < n)
        def _():
            st_copy(d).wait_send()

    kv_each(me, True, lambda copy: copy.wait_send())

    def forwarded(k, carry):
        kv_each(me - 2 * k, False, lambda copy: copy.wait_send())
        return carry

    lax.fori_loop(1, me // 2 + 1, forwarded, 0)


def leave(hy_v, at_v, hy_out, at_out, sem):
    copies = [pltpu.make_async_copy(hy_v, hy_out, sem.at[0]),
              pltpu.make_async_copy(at_v, at_out, sem.at[1])]
    for copy in copies:
        copy.start()
    for copy in copies:
        copy.wait()


def body(n, streams, short_taps, modal_residue, modal_rate, skip_gain, queries, keys, values):
    rows, _, chans = streams.shape
    heads, size = queries.shape[1], queries.shape[2]
    modes, groups = modal_rate.shape
    tiles = chans // LANES
    per = LANES // GSIZE
    wide = heads * rows
    chunk = min(256, wide)
    reach = short_taps.shape[0]
    vmem, hbm = pl.BlockSpec(memory_space=pltpu.VMEM), pl.BlockSpec(memory_space=pltpu.HBM)
    dma = pltpu.SemaphoreType.DMA
    hyena, attn = pl.pallas_call(
        functools.partial(kernel, n, heads, chunk),
        out_shape=(jax.ShapeDtypeStruct((rows, chans), BF16),
                   jax.ShapeDtypeStruct((wide, size), BF16)),
        in_specs=[hbm] * 8,
        out_specs=(vmem, vmem),
        scratch_shapes=[
            pltpu.VMEM((3, reach, groups), F32),
            pltpu.VMEM((modes, groups), F32),
            pltpu.VMEM((modes, groups), F32),
            pltpu.VMEM((chans,), F32),
            pltpu.VMEM((3, rows, chans), BF16),
            pltpu.VMEM((wide, size), BF16),
            pltpu.VMEM((n, 2, rows, size), BF16),
            pltpu.VMEM((2 * EDGE, chans + chans // 2), BF16),
            pltpu.VMEM((2 * EDGE, chans + chans // 2), BF16),
            pltpu.VMEM((3 * tiles, rows + EDGE, LANES), F32),
            pltpu.VMEM((rows, chans), BF16),
            pltpu.VMEM((3 * EDGE + 2 * modes, groups), F32),
            pltpu.VMEM((modes, chans), F32),
            pltpu.VMEM((modes, chans), F32),
            pltpu.VMEM((EDGE, chans), F32),
            pltpu.VMEM((3, EDGE, chans), F32),
            pltpu.VMEM((tiles, LANES, LANES), F32),
            pltpu.VMEM((tiles, LANES, LANES), BF16),
            pltpu.VMEM((tiles, LANES, LANES), BF16),
            pltpu.VMEM((rows, chans), F32),
            pltpu.VMEM((rows, chans), F32),
            pltpu.VMEM((modes, chans), BF16),
            pltpu.VMEM((n, modes, chans), BF16),
            pltpu.VMEM((size + EDGE, wide), F32),
            pltpu.VMEM((EDGE, wide), F32),
            dma((8,)), dma((n, 2, 2)), dma((n, 2)),
            dma, dma, dma((n,)), dma((n,)),
        ],
        compiler_params=pltpu.CompilerParams(
            collective_id=0, has_side_effects=True, vmem_limit_bytes=40 * 1024 * 1024),
        name="mixers",
    )(*[pltpu.with_memory_space_constraint(x, pltpu.HBM) for x in (
        jnp.transpose(streams, (1, 0, 2)),
        jnp.transpose(short_taps, (1, 0, 2)),
        modal_residue,
        modal_rate,
        skip_gain,
        queries.reshape(wide, size),
        keys.reshape(rows, size),
        values.reshape(rows, size),
    )])
    hyena, attn = pl.pallas_call(
        leave,
        out_shape=(jax.ShapeDtypeStruct((rows, chans), BF16),
                   jax.ShapeDtypeStruct((wide, size), BF16)),
        in_specs=[vmem, vmem],
        out_specs=(hbm, hbm),
        scratch_shapes=[dma((2,))],
        compiler_params=pltpu.CompilerParams(vmem_limit_bytes=2 * 1024 * 1024),
        name="leave",
    )(hyena, attn)
    return hyena, attn.reshape(rows, heads, size)


def solution(mesh):
    in_specs = (
        P(("dp", "ctx"), None, "mp"),
        P(None, None, "mp"),
        P(None, "mp"),
        P(None, "mp"),
        P("mp"),
        P(("dp", "ctx"), "mp", None),
        P(("dp", "ctx"), "mp", None),
        P(("dp", "ctx"), "mp", None),
    )
    out_specs = (P(("dp", "ctx"), "mp"), P(("dp", "ctx"), "mp", None))
    return jax.shard_map(functools.partial(body, mesh.shape["ctx"]), mesh=mesh,
                         in_specs=in_specs, out_specs=out_specs, check_vma=False)
```
